32 devices in a mesh: cube: 4 (over x, core), blk: 8 (over z, y).
Axes of the slice: x: 2, y: 2, z: 4, core: 2. Of those that a mesh axis runs over, the one named last changes fastest.
Arguments:
- right_side: float32 [3, 4, 8, 32, 64], P(None, 'cube', 'blk'), may hold values from -6 to 6
- diag_inverse: float32 [896, 2048], P('cube', 'blk'), as said below
- panels: float32 [2, 4, 8, 2, 16, 32], P(None, 'cube', 'blk'), may hold values from -1 to 1
- extend_map: int32 [2, 4, 8, 2, 16], P(None, 'cube', 'blk'), may hold values from 0 to 31
Outputs:
- solution: float32 [3, 4, 8, 32, 64], P(None, 'cube', 'blk')
The draws below stay inside these ranges and needn't reach their ends.
Inputs may be any that keep to these rules, and one draw needn't show every extreme that they name: `extend_map`: each entry names one of the 32 parent rows held by the receiving device. `diag_inverse`: dense real entries.
All inputs are finite; a program needn't handle non-finite values.
Results may differ from the reference program's by a relative error of at most 0.0001.
Values sent between devices are 32-bit elements; how exact they have to be, the bound alone decides.
No kernel may reach another device: no remote copies, remote signals or barrier semaphores. Data moves between devices by JAX's collectives and lax.ppermute only.
A program may use at most 64 MiB of HBM per device.

```python
import jax
import jax.numpy as jnp
from jax import lax

K = 64
ROWS_DEV = 32
UPD_ROWS = 16
LEVELS = 3
N_CUBE = 4
N_BLK = 8


def draw_diag_inverse(key, part):
    total_rows = N_CUBE * (2 ** LEVELS - 1) * ROWS_DEV
    total_cols = N_BLK * N_BLK * ROWS_DEV
    base = jax.random.normal(key, (total_rows, total_cols), jnp.float32)
    local_block = jnp.arange(total_rows, dtype=jnp.int32) % ((2 ** LEVELS - 1) * ROWS_DEV) // ROWS_DEV
    level_ids = jnp.zeros((total_rows,), jnp.int32)
    for marker in range(1, LEVELS):
        level_ids = level_ids + (local_block >= 2 ** marker - 1).astype(jnp.int32)
    node_rows = N_BLK * ROWS_DEV * jnp.exp2(level_ids.astype(jnp.float32))
    return base * lax_rsqrt(node_rows)[:, None]


def lax_rsqrt(values):
    return 1.0 / jnp.sqrt(values)


def touch_ends(array, rng, smallest, top_value):
    shape = array.shape
    place = [jax.random.randint(jax.random.fold_in(rng, axis), (), 0, shape[axis]) for axis in range(len(shape))]
    array = array.at[tuple(place)].set(smallest)
    longest = shape.index(max(shape))
    place[longest] = (place[longest] + 1) % shape[longest]
    return array.at[tuple(place)].set(top_value)


def block_scale(rng, extent, shards, low, largest):
    loudness = 1.0
    for position, shards_of in shards:
        steps = jax.random.uniform(jax.random.fold_in(jax.random.fold_in(rng, 6), position), (shards_of,), jnp.float32, low / len(shards), largest / len(shards))
        loudness = loudness * jnp.repeat(jnp.exp(steps), extent[position] // shards_of).reshape((-1,) + (1,) * (len(extent) - 1 - position))
    return loudness


def bell_draw(rng, dims, deviation, reach, pieces=(), kind=jnp.bfloat16):
    factor_of = block_scale(rng, dims, pieces, -0.22, 0.18) if pieces else 1.0
    result = jax.random.normal(rng, dims, jnp.float32) * deviation * factor_of
    return jnp.minimum(jnp.maximum(result, -reach), reach).astype(kind)


def setup_inputs(seed: int = 0) -> dict:
    arg_keys = jax.random.split(jax.random.key(seed), 5)
    return {
        "right_side": bell_draw(arg_keys[0], (LEVELS, N_CUBE, N_BLK, ROWS_DEV, K), 1.0, 6.0, ((1, 4), (2, 8)), jnp.float32),
        "diag_inverse": draw_diag_inverse(jax.random.fold_in(arg_keys[4], 71), 0),
        "panels": bell_draw(arg_keys[2], (LEVELS - 1, N_CUBE, N_BLK, 2, UPD_ROWS, ROWS_DEV), ROWS_DEV ** -0.5, 1.0, ((1, 4), (2, 8)), jnp.float32),
        "extend_map": touch_ends(jax.random.randint(arg_keys[3], (LEVELS - 1, N_CUBE, N_BLK, 2, UPD_ROWS), 0, ROWS_DEV), jax.random.fold_in(arg_keys[3], 1), 0, ROWS_DEV - 1).astype(jnp.int32),
    }


def reference(right_side, diag_inverse, panels, extend_map):
    highest = lax.Precision.HIGHEST
    cube_ids = jnp.arange(N_CUBE, dtype=jnp.int32)
    row_ids = jnp.arange(ROWS_DEV, dtype=jnp.int32)
    inverse_table = diag_inverse.reshape(N_CUBE, (2 ** LEVELS - 1) * ROWS_DEV, N_BLK, N_BLK, ROWS_DEV)
    update = jnp.zeros((N_CUBE, N_BLK, ROWS_DEV, K), jnp.float32)
    solved = []
    onehots = []
    diag_levels = []
    for tree_level in range(LEVELS):
        group_width = 2 ** tree_level
        group_count = N_CUBE // group_width
        offset = (group_width - 1) * ROWS_DEV
        diag_level = inverse_table[:, offset:offset + group_width * ROWS_DEV].reshape(
            group_count, group_width, group_width, ROWS_DEV, N_BLK, N_BLK, ROWS_DEV)
        diag_levels.append(diag_level)
        residual_rows = right_side[tree_level] - update
        grouped = residual_rows.reshape(group_count, group_width, N_BLK, ROWS_DEV, K)
        solved_rows = jnp.einsum("gjpsqbr,gpqsk->gjbrk", diag_level, grouped, precision=highest)
        solved_rows = solved_rows.reshape(N_CUBE, N_BLK, ROWS_DEV, K)
        solved.append(solved_rows)
        if tree_level + 1 < LEVELS:
            onehot = (extend_map[tree_level][..., None] == row_ids).astype(jnp.float32)
            onehots.append(onehot)
            upd_rows = jnp.einsum("cbhmr,cbrk->cbhmk", panels[tree_level], solved_rows, precision=highest)
            extended = jnp.einsum("cbhmt,cbhmk->cbhtk", onehot, upd_rows, precision=highest)
            partner = jnp.bitwise_xor(cube_ids, group_width)
            update = extended[:, :, 0] + extended[partner][:, :, 1]
    results = [None] * LEVELS
    parent = None
    for tree_level in reversed(range(LEVELS)):
        group_width = 2 ** tree_level
        group_count = N_CUBE // group_width
        work_rows = solved[tree_level]
        if parent is not None:
            partner = jnp.bitwise_xor(cube_ids, group_width)
            parent_pair = jnp.stack([parent, parent[partner]], axis=2)
            fetched = jnp.einsum("cbhmt,cbhtk->cbhmk", onehots[tree_level], parent_pair, precision=highest)
            work_rows = work_rows - jnp.einsum("cbhmr,cbhmk->cbrk", panels[tree_level], fetched, precision=highest)
        grouped = work_rows.reshape(group_count, group_width, N_BLK, ROWS_DEV, K)
        answer = jnp.einsum("gjpsqbr,gjbrk->gpqsk", diag_levels[tree_level], grouped, precision=highest)
        parent = answer.reshape(N_CUBE, N_BLK, ROWS_DEV, K)
        results[tree_level] = parent
    return jnp.stack(results)
```

```python
import jax
import jax.numpy as jnp
from jax import lax
from jax.sharding import PartitionSpec as P

HIGHEST = lax.Precision.HIGHEST
GATHER_BYTES = 8 * 2**20


def swap(block, axis, mask):
    count = lax.axis_size(axis)
    return lax.ppermute(block, axis, [(i, i ^ mask) for i in range(count)])


def gather_rows(block):
    count = lax.axis_size("blk")
    if count == 1:
        return [block]
    half = count // 2
    far = swap(block, "blk", half)
    near = {m: swap(block, "blk", m) for m in reversed(range(1, half))}
    out = {0: block, half: far}
    for m in reversed(range(1, half)):
        out[m] = near[m]
        out[m + half] = swap(far, "blk", m)
    return [out[m] for m in range(count)]


def by_bits(parts, index):
    bit = 1
    while bit < len(parts):
        side = (index // bit) % 2 == 1
        parts = [jnp.where(side, parts[j ^ bit], parts[j]) for j in range(len(parts))]
        bit *= 2
    return parts


def gathered(right_side, diag_inverse, panels, extend_map):
    levels, _, _, rows, cols = right_side.shape
    width = diag_inverse.shape[1]
    n_blk = lax.axis_size("blk")
    cube = lax.axis_index("cube")
    me = lax.axis_index("blk")
    row_ids = jnp.arange(rows, dtype=jnp.int32)
    onehot = (extend_map[:, 0, 0][..., None] == row_ids).astype(jnp.float32)
    extend = jnp.einsum("lhmt,lhmr->tlhr", onehot, panels[:, 0, 0], precision=HIGHEST)
    vectors = jnp.transpose(right_side[:, 0, 0], (1, 0, 2)).reshape(rows, levels * cols)
    packed = jnp.concatenate([vectors, extend.reshape(rows, -1)], axis=1)
    pad = -packed.size % width
    packed = jnp.pad(packed.reshape(-1), (0, pad)).reshape(-1, width)
    top = (2 ** (levels - 1) - 1) * rows
    first = gather_rows(jnp.concatenate([diag_inverse[:top], packed], axis=0))
    last = gather_rows(diag_inverse[top:])

    small = jnp.stack([f[top:] for f in first]).reshape(n_blk, -1)[:, : small_size(rows, levels, cols)]
    small = small.reshape(n_blk, rows, -1)
    rhs = [
        small[:, :, l * cols : (l + 1) * cols].reshape(n_blk * rows, cols) for l in range(levels)
    ]
    ext = small[:, :, levels * cols :].reshape(n_blk, rows, levels - 1, 2, rows)
    ext = jnp.transpose(ext, (2, 3, 0, 1, 4))
    same = (jnp.arange(n_blk) ^ me)[:, None] == jnp.arange(n_blk)[None, :]
    ext = jnp.where(
        same[None, None, :, None, :, None], ext[:, :, :, :, None, :], 0.0
    ).reshape(levels - 1, 2 * n_blk * rows, n_blk * rows)

    def diag_of(l):
        span = 2**l
        if l == levels - 1:
            pieces = [p.reshape(span, 1, rows, width) for p in last]
        else:
            low = (span - 1) * rows
            pieces = [p[low : low + span * rows].reshape(span, 1, rows, width) for p in first]
        return jnp.concatenate(pieces, axis=1).reshape(span * n_blk * rows, width)

    node = n_blk * rows
    diags = [diag_of(l) for l in range(levels)]
    z = rhs[0]
    ys = []
    for l in range(levels):
        y = jnp.einsum("ab,ak->bk", diags[l], z, precision=HIGHEST)
        ys.append(y)
        if l + 1 < levels:
            e = jnp.einsum("ab,bk->ak", ext[l], y, precision=HIGHEST)
            mine = rhs[l + 1] - e[:node]
            other = e[node:]
            got = swap(jnp.concatenate([mine, other], axis=0), "cube", 2**l)
            parts = {0: mine - got[node:], 2**l: got[:node] - other}
            for j in reversed(range(l)):
                keys = list(parts)
                got = swap(jnp.concatenate([parts[k] for k in keys], axis=0), "cube", 2**j)
                for i, k in enumerate(keys):
                    parts[k ^ 2**j] = got[i * node : (i + 1) * node]
            order = by_bits([parts[k] for k in range(2 ** (l + 1))], cube)
            z = jnp.concatenate(order, axis=0)
    outs = [None] * levels
    w = ys[-1]
    for l in reversed(range(levels)):
        if l == 0:
            own = diags[0][:rows]
            outs[0] = jnp.einsum("ab,bk->ak", own, w, precision=HIGHEST)
            break
        x = jnp.einsum("ab,bk->ak", diags[l], w, precision=HIGHEST)
        order = by_bits([x[p * node : (p + 1) * node] for p in range(2**l)], cube)
        held = {k: order[k] for k in range(2**l)}
        for j in range(l - 1):
            keep = [k for k in held if not k & 2**j]
            got = swap(jnp.concatenate([held[k ^ 2**j] for k in keep], axis=0), "cube", 2**j)
            held = {k: held[k] + got[i * node : (i + 1) * node] for i, k in enumerate(keep)}
        bit = 2 ** (l - 1)
        got = swap(jnp.concatenate([held[bit], held[0]], axis=0), "cube", bit)
        pair = jnp.concatenate([held[0], held[bit]], axis=0) + got
        outs[l] = pair[:rows]
        w = ys[l - 1] - jnp.einsum("ab,ak->bk", ext[l - 1], pair, precision=HIGHEST)
    return jnp.stack(outs)[:, None, None]


def small_size(rows, levels, cols):
    return rows * (levels * cols + (levels - 1) * 2 * rows)


def from_partner(block, axis, apart):
    count = lax.axis_size(axis)
    route = []
    for low in range(count):
        high = low | 1 << apart
        if high != low and high < count:
            route += [(low, high), (high, low)]
    return lax.ppermute(block, axis, route)


def collect_pairs(residual_rows, tree_level, cube_index):
    gathered = residual_rows
    for bit_index in range(tree_level):
        partner_rows = from_partner(gathered, "cube", bit_index)
        lower_side = cube_index // 2**bit_index % 2 == 0
        gathered = jnp.where(
            lower_side,
            jnp.concatenate([gathered, partner_rows], axis=0),
            jnp.concatenate([partner_rows, gathered], axis=0),
        )
    return gathered


def reduce_pairs(partial_value, tree_level, cube_index):
    for bit_index in reversed(range(tree_level)):
        half_rows = partial_value.shape[0] // 2
        lower_rows = partial_value[:half_rows]
        upper_rows = partial_value[half_rows:]
        lower_side = cube_index // 2**bit_index % 2 == 0
        kept_rows = jnp.where(lower_side, lower_rows, upper_rows)
        sent_rows = jnp.where(lower_side, upper_rows, lower_rows)
        partial_value = kept_rows + from_partner(sent_rows, "cube", bit_index)
    return partial_value


def stepwise(right_side, diag_inverse, panels, extend_map):
    highest = lax.Precision.HIGHEST
    levels = right_side.shape[0]
    local_rows = right_side.shape[3]
    columns_k = right_side.shape[4]
    cube_index = lax.axis_index("cube")
    rhs_rows = right_side[:, 0, 0]
    panel_blocks = panels[:, 0, 0]
    row_maps = extend_map[:, 0, 0]
    row_ids = jnp.arange(local_rows, dtype=jnp.int32)
    update = jnp.zeros((local_rows, columns_k), jnp.float32)
    solved = []
    onehots = []
    diag_blocks = []
    for tree_level in range(levels):
        span_rows = 2**tree_level * local_rows
        offset = (2**tree_level - 1) * local_rows
        diag_block = diag_inverse[offset : offset + span_rows]
        diag_blocks.append(diag_block)
        residual_rows = rhs_rows[tree_level] - update
        column = collect_pairs(residual_rows, tree_level, cube_index)

        def term_rows(first_row, row_count, diag_block=diag_block, column=column):
            return jnp.einsum("ir,ik->rk", diag_block, column, precision=highest)

        solved_rows = lax.psum_scatter(
            term_rows(jnp.int32(0), lax.axis_size("blk") * local_rows),
            "blk",
            scatter_dimension=0,
            tiled=True,
        )
        solved.append(solved_rows)
        if tree_level + 1 < levels:
            onehot = (row_maps[tree_level][..., None] == row_ids).astype(jnp.float32)
            onehots.append(onehot)
            upd_rows = jnp.einsum(
                "hmr,rk->hmk", panel_blocks[tree_level], solved_rows, precision=highest
            )
            extended = jnp.einsum("hmt,hmk->htk", onehot, upd_rows, precision=highest)
            update = extended[0] + from_partner(extended[1], "cube", tree_level)
    results = [None] * levels
    parent = None
    for tree_level in reversed(range(levels)):
        span_rows = 2**tree_level * local_rows
        diag_block = diag_blocks[tree_level]
        work_rows = solved[tree_level]
        if parent is not None:
            partner_rows = from_partner(parent, "cube", tree_level)
            parent_pair = jnp.stack([parent, partner_rows], axis=0)
            fetched = jnp.einsum(
                "hmt,htk->hmk", onehots[tree_level], parent_pair, precision=highest
            )
            work_rows = work_rows - jnp.einsum(
                "hmr,hmk->rk", panel_blocks[tree_level], fetched, precision=highest
            )

        def accumulate(running, shard_rows, first_row, diag_block=diag_block):
            return jnp.einsum("ir,rk->ik", diag_block, shard_rows, precision=highest)

        initial = jnp.zeros((span_rows, columns_k), jnp.float32)
        partial_value = accumulate(
            initial, lax.all_gather(work_rows, "blk", axis=0, tiled=True), jnp.int32(0)
        )
        parent = reduce_pairs(partial_value, tree_level, cube_index)
        results[tree_level] = parent
    return jnp.stack(results)[:, None, None]


def body(right_side, diag_inverse, panels, extend_map):
    if lax.axis_size("blk") * diag_inverse.size * 4 > GATHER_BYTES:
        return stepwise(right_side, diag_inverse, panels, extend_map)
    return gathered(right_side, diag_inverse, panels, extend_map)


def solution(mesh):
    placed = (
        P(None, "cube", "blk", None, None),
        P("cube", "blk"),
        P(None, "cube", "blk", None, None, None),
        P(None, "cube", "blk", None, None),
    )
    return jax.shard_map(
        body,
        mesh=mesh,
        in_specs=placed,
        out_specs=P(None, "cube", "blk", None, None),
        check_vma=False,
    )
```

```python
import functools

import jax
import jax.numpy as jnp
from jax import lax
from jax.experimental import pallas as pl
from jax.experimental.pallas import tpu as pltpu
from jax.sharding import PartitionSpec as P

HIGHEST = lax.Precision.HIGHEST
GATHER_BYTES = 8 * 2**20


def dot(a, b):
    return lax.dot_general(
        a, b, (((1,), (0,)), ((), ())), precision=HIGHEST, preferred_element_type=jnp.float32
    )


def dot_t(a, b):
    return lax.dot_general(
        a, b, (((0,), (0,)), ((), ())), precision=HIGHEST, preferred_element_type=jnp.float32
    )


def swap(block, axis, mask):
    count = lax.axis_size(axis)
    return lax.ppermute(block, axis, [(i, i ^ mask) for i in range(count)])


def gather_rows(block):
    half = lax.axis_size("blk") // 2
    far = swap(block, "blk", half)
    near = {m: swap(block, "blk", m) for m in reversed(range(1, half))}
    out = {0: block, half: far}
    for m in reversed(range(1, half)):
        out[m] = near[m]
        out[m + half] = swap(far, "blk", m)
    return [out[m] for m in range(2 * half)]


class Packing:
    def __init__(self, levels, rows, cols, width, n_blk):
        self.levels, self.rows, self.cols, self.width, self.n_blk = levels, rows, cols, width, n_blk
        self.top = (2 ** (levels - 1) - 1) * rows
        self.low = (levels - 1) * (cols + 2 * rows)
        self.fold = width // cols
        self.fits = (
            self.low == width
            and width == n_blk * rows
            and rows % (8 * self.fold) == 0
            and n_blk == 2 ** (n_blk.bit_length() - 1)
        )
        self.height = self.top + rows + rows // self.fold

    def rhs(self, piece, level):
        rows, cols = self.rows, self.cols
        if level < self.levels - 1:
            return piece[self.top : self.top + rows, level * cols : (level + 1) * cols]
        start, step = self.top + rows, rows // self.fold
        return jnp.concatenate(
            [piece[start : start + step, j * cols : (j + 1) * cols] for j in range(self.fold)], axis=0
        )

    def extend(self, piece, level):
        rows = self.rows
        first = (self.levels - 1) * self.cols + level * 2 * rows
        return jnp.concatenate(
            [piece[self.top : self.top + rows, first + h * rows : first + (h + 1) * rows] for h in (0, 1)],
            axis=0,
        )

    def diag(self, pieces, level, first=None):
        first = (2**level - 1) * self.rows if first is None else first
        return jnp.concatenate(
            [
                q[first + p * self.rows : first + (p + 1) * self.rows, :]
                for p in range(2**level)
                for q in pieces
            ],
            axis=0,
        )


def pack_kernel(pk, rhs_ref, panels_ref, maps_ref, diag_ref, out_ref):
    rows, cols = pk.rows, pk.cols
    out_ref[: pk.top, :] = diag_ref[: pk.top, :]
    parts = [rhs_ref[l] for l in range(pk.levels - 1)]
    for l in range(pk.levels - 1):
        for h in (0, 1):
            panel = panels_ref[l, h]
            row_ids = lax.broadcasted_iota(jnp.int32, (rows, panel.shape[0]), 0)
            names = maps_ref[2 * l + h : 2 * l + h + 1, :]
            onehot = jnp.where(row_ids == names, 1.0, 0.0).astype(jnp.float32)
            parts.append(dot(onehot, panel))
    out_ref[pk.top : pk.top + rows, :] = jnp.concatenate(parts, axis=1)
    last = rhs_ref[pk.levels - 1]
    step = rows // pk.fold
    out_ref[pk.top + rows :, :] = jnp.concatenate(
        [last[j * step : (j + 1) * step] for j in range(pk.fold)], axis=1
    )


def block_of(pk, m):
    place = (lax.axis_index("blk") ^ m) * pk.rows
    return pl.ds(pl.multiple_of(place, pk.rows), pk.rows)


def extend_out(pk, level, pieces, y_ref, send_ref):
    rows, node = pk.rows, pk.width
    for m, piece in enumerate(pieces):
        e = dot(pk.extend(piece, level), y_ref[block_of(pk, m), :])
        send_ref[m * rows : (m + 1) * rows, :] = pk.rhs(piece, level + 1) - e[:rows]
        send_ref[node + m * rows : node + (m + 1) * rows, :] = e[rows:]


def first_kernel(pk, *refs):
    pieces, (send_ref, y_ref) = refs[: pk.n_blk], refs[pk.n_blk :]
    z = jnp.concatenate([pk.rhs(q, 0) for q in pieces], axis=0)
    y_ref[...] = dot_t(pk.diag(pieces, 0), z)
    extend_out(pk, 0, pieces, y_ref, send_ref)


def middle_kernel(pk, *refs):
    pieces, (mine_ref, got_ref, send_ref, y_ref) = refs[: pk.n_blk], refs[pk.n_blk :]
    node = pk.width
    own = mine_ref[:node] - got_ref[node:]
    other = got_ref[:node] - mine_ref[node:]
    upper = lax.axis_index("cube") % 2 == 1
    z = jnp.concatenate([jnp.where(upper, other, own), jnp.where(upper, own, other)], axis=0)
    y_ref[...] = dot_t(pk.diag(pieces, 1), z)
    extend_out(pk, 1, pieces, y_ref, send_ref)


def top_kernel(pk, *refs):
    pieces, (mine_ref, got_ref, keep_ref, send_ref, vec_ref) = refs[: pk.n_blk], refs[pk.n_blk :]
    node = pk.width
    cube = lax.axis_index("cube")

    def part(k):
        return pl.ds(pl.multiple_of((cube ^ k) * node, node), node)

    vec_ref[part(0), :] = mine_ref[:node]
    vec_ref[part(2), :] = mine_ref[node:]
    vec_ref[part(1), :] = got_ref[:node]
    vec_ref[part(3), :] = got_ref[node:]
    diag = pk.diag(pieces, 2, 0)
    vec_ref[...] = dot(diag, dot_t(diag, vec_ref[...]))
    keep_ref[:node] = vec_ref[part(0), :]
    keep_ref[node:] = vec_ref[part(2), :]
    send_ref[:node] = vec_ref[part(1), :]
    send_ref[node:] = vec_ref[part(3), :]


def reduce_rows(pk, level, pieces, y_ref, pair, w_ref):
    rows, node = pk.rows, pk.width
    for m, piece in enumerate(pieces):
        both = jnp.concatenate(
            [pair[m * rows : (m + 1) * rows], pair[node + m * rows : node + (m + 1) * rows]], axis=0
        )
        place = block_of(pk, m)
        w_ref[place, :] = y_ref[place, :] - dot_t(pk.extend(piece, level), both)


def down_kernel(pk, *refs):
    pieces, (y_ref, mine_ref, got_ref, keep_ref, send_ref, top_ref, w_ref) = refs[: pk.n_blk], refs[pk.n_blk :]
    node = pk.width
    pair = mine_ref[...] + got_ref[...]
    top_ref[...] = pair[: pk.rows]
    reduce_rows(pk, 1, pieces, y_ref, pair, w_ref)
    x = dot(pk.diag(pieces, 1), w_ref[...])
    upper = lax.axis_index("cube") % 2 == 1
    own = jnp.where(upper, x[node:], x[:node])
    other = jnp.where(upper, x[:node], x[node:])
    keep_ref[:node] = own
    keep_ref[node:] = other
    send_ref[:node] = other
    send_ref[node:] = own


def last_kernel(pk, *refs):
    pieces, (y_ref, mine_ref, got_ref, top_ref, out_ref, w_ref) = refs[: pk.n_blk], refs[pk.n_blk :]
    pair = mine_ref[...] + got_ref[...]
    out_ref[2] = top_ref[...]
    out_ref[1] = pair[: pk.rows]
    reduce_rows(pk, 0, pieces, y_ref, pair, w_ref)
    out_ref[0] = dot(pieces[0][: pk.rows, :], w_ref[...])


def call(kernel, pk, args, outs, scratch=()):
    vmem = pl.BlockSpec(memory_space=pltpu.VMEM)
    return pl.pallas_call(
        functools.partial(kernel, pk),
        out_shape=[jax.ShapeDtypeStruct(s, jnp.float32) for s in outs],
        in_specs=[vmem] * len(args),
        out_specs=[vmem] * len(outs),
        scratch_shapes=[pltpu.VMEM(s, jnp.float32) for s in scratch],
        compiler_params=pltpu.CompilerParams(vmem_limit_bytes=24 * 2**20),
    )(*args)


def gathered(pk, right_side, diag_inverse, panels, extend_map):
    rows, cols, node = pk.rows, pk.cols, pk.width
    one, two = (node, cols), (2 * node, cols)
    maps = extend_map.reshape(-1, extend_map.shape[-1])
    (packed,) = call(
        pack_kernel,
        pk,
        [right_side[:, 0, 0], panels[:, 0, 0], maps, diag_inverse],
        [(pk.height, pk.width)],
    )
    first = gather_rows(packed)
    last = gather_rows(diag_inverse[pk.top :])

    send, y0 = call(first_kernel, pk, first, [two, one])
    got = swap(send, "cube", 1)
    send, y1 = call(middle_kernel, pk, [*first, send, got], [two, one])
    got = swap(send, "cube", 2)
    held = jnp.concatenate([send[:node] - got[node:], got[:node] - send[node:]], axis=0)
    got = swap(held, "cube", 1)
    keep, send = call(top_kernel, pk, [*last, held, got], [two, two], [(4 * node, cols)])
    held = keep + swap(send, "cube", 1)
    got = swap(jnp.concatenate([held[node:], held[:node]], axis=0), "cube", 2)
    keep, send, top = call(down_kernel, pk, [*first, y1, held, got], [two, two, (rows, cols)], [one])
    got = swap(send, "cube", 1)
    (out,) = call(last_kernel, pk, [*first, y0, keep, got, top], [(3, rows, cols)], [one])
    return out[:, None, None]


def from_partner(block, axis, apart):
    count = lax.axis_size(axis)
    route = []
    for low in range(count):
        high = low | 1 << apart
        if high != low and high < count:
            route += [(low, high), (high, low)]
    return lax.ppermute(block, axis, route)


def collect_pairs(residual_rows, tree_level, cube_index):
    gathered = residual_rows
    for bit_index in range(tree_level):
        partner_rows = from_partner(gathered, "cube", bit_index)
        lower_side = cube_index // 2**bit_index % 2 == 0
        gathered = jnp.where(
            lower_side,
            jnp.concatenate([gathered, partner_rows], axis=0),
            jnp.concatenate([partner_rows, gathered], axis=0),
        )
    return gathered


def reduce_pairs(partial_value, tree_level, cube_index):
    for bit_index in reversed(range(tree_level)):
        half_rows = partial_value.shape[0] // 2
        lower_rows = partial_value[:half_rows]
        upper_rows = partial_value[half_rows:]
        lower_side = cube_index // 2**bit_index % 2 == 0
        kept_rows = jnp.where(lower_side, lower_rows, upper_rows)
        sent_rows = jnp.where(lower_side, upper_rows, lower_rows)
        partial_value = kept_rows + from_partner(sent_rows, "cube", bit_index)
    return partial_value


def stepwise(right_side, diag_inverse, panels, extend_map):
    highest = lax.Precision.HIGHEST
    levels = right_side.shape[0]
    local_rows = right_side.shape[3]
    columns_k = right_side.shape[4]
    cube_index = lax.axis_index("cube")
    rhs_rows = right_side[:, 0, 0]
    panel_blocks = panels[:, 0, 0]
    row_maps = extend_map[:, 0, 0]
    row_ids = jnp.arange(local_rows, dtype=jnp.int32)
    update = jnp.zeros((local_rows, columns_k), jnp.float32)
    solved = []
    onehots = []
    diag_blocks = []
    for tree_level in range(levels):
        span_rows = 2**tree_level * local_rows
        offset = (2**tree_level - 1) * local_rows
        diag_block = diag_inverse[offset : offset + span_rows]
        diag_blocks.append(diag_block)
        residual_rows = rhs_rows[tree_level] - update
        column = collect_pairs(residual_rows, tree_level, cube_index)

        def term_rows(first_row, row_count, diag_block=diag_block, column=column):
            return jnp.einsum("ir,ik->rk", diag_block, column, precision=highest)

        solved_rows = lax.psum_scatter(
            term_rows(jnp.int32(0), lax.axis_size("blk") * local_rows),
            "blk",
            scatter_dimension=0,
            tiled=True,
        )
        solved.append(solved_rows)
        if tree_level + 1 < levels:
            onehot = (row_maps[tree_level][..., None] == row_ids).astype(jnp.float32)
            onehots.append(onehot)
            upd_rows = jnp.einsum(
                "hmr,rk->hmk", panel_blocks[tree_level], solved_rows, precision=highest
            )
            extended = jnp.einsum("hmt,hmk->htk", onehot, upd_rows, precision=highest)
            update = extended[0] + from_partner(extended[1], "cube", tree_level)
    results = [None] * levels
    parent = None
    for tree_level in reversed(range(levels)):
        span_rows = 2**tree_level * local_rows
        diag_block = diag_blocks[tree_level]
        work_rows = solved[tree_level]
        if parent is not None:
            partner_rows = from_partner(parent, "cube", tree_level)
            parent_pair = jnp.stack([parent, partner_rows], axis=0)
            fetched = jnp.einsum(
                "hmt,htk->hmk", onehots[tree_level], parent_pair, precision=highest
            )
            work_rows = work_rows - jnp.einsum(
                "hmr,hmk->rk", panel_blocks[tree_level], fetched, precision=highest
            )

        def accumulate(running, shard_rows, first_row, diag_block=diag_block):
            return jnp.einsum("ir,rk->ik", diag_block, shard_rows, precision=highest)

        initial = jnp.zeros((span_rows, columns_k), jnp.float32)
        partial_value = accumulate(
            initial, lax.all_gather(work_rows, "blk", axis=0, tiled=True), jnp.int32(0)
        )
        parent = reduce_pairs(partial_value, tree_level, cube_index)
        results[tree_level] = parent
    return jnp.stack(results)[:, None, None]

def body(right_side, diag_inverse, panels, extend_map):
    levels, _, _, rows, cols = right_side.shape
    n_blk = lax.axis_size("blk")
    pk = Packing(levels, rows, cols, diag_inverse.shape[1], n_blk)
    small = n_blk * diag_inverse.size * 4 <= GATHER_BYTES
    if levels == 3 and lax.axis_size("cube") == 4 and pk.fits and small:
        return gathered(pk, right_side, diag_inverse, panels, extend_map)
    return stepwise(right_side, diag_inverse, panels, extend_map)


def solution(mesh):
    placed = (
        P(None, "cube", "blk", None, None),
        P("cube", "blk"),
        P(None, "cube", "blk", None, None, None),
        P(None, "cube", "blk", None, None),
    )
    return jax.shard_map(
        body,
        mesh=mesh,
        in_specs=placed,
        out_specs=P(None, "cube", "blk", None, None),
        check_vma=False,
    )
```

```python
import functools

import jax
import jax.numpy as jnp
from jax import lax
from jax.experimental import pallas as pl
from jax.experimental.pallas import tpu as pltpu
from jax.sharding import PartitionSpec as P

HIGHEST = lax.Precision.HIGHEST
GATHER_BYTES = 8 * 2**20


def dot(a, b):
    return lax.dot_general(
        a, b, (((1,), (0,)), ((), ())), precision=HIGHEST, preferred_element_type=jnp.float32
    )


def dot_t(a, b):
    return lax.dot_general(
        a, b, (((0,), (0,)), ((), ())), precision=HIGHEST, preferred_element_type=jnp.float32
    )


def swap(block, axis, mask):
    count = lax.axis_size(axis)
    return lax.ppermute(block, axis, [(i, i ^ mask) for i in range(count)])


def ring_place(blk, count):
    return jnp.where(blk % 2 == 0, blk // 2, count - 1 - blk // 2)


def ring_group(place, count):
    return jnp.where(place < count // 2, 2 * place, 2 * (count - 1 - place) + 1)


def ring_step(block):
    cubes, count = lax.axis_size("cube"), lax.axis_size("blk")
    order = list(range(0, count, 2)) + list(range(count - 1, 0, -2))
    route = [
        (c * count + order[i], c * count + order[(i + 1 - 2 * (c % 2)) % count])
        for c in range(cubes)
        for i in range(count)
    ]
    return lax.ppermute(block, ("cube", "blk"), route)


def ring_offsets(count):
    return [0] + [x for r in range(1, count // 2) for x in (r, -r)] + [count // 2]


def gather_rows(block):
    height = block.shape[0]
    moving = jnp.concatenate([block, swap(block, "cube", 1)], axis=0)
    out = [block]
    for _ in range(1, lax.axis_size("blk") // 2):
        moving = ring_step(moving)
        out += [moving[:height], swap(moving[height:], "cube", 1)]
    return out + [ring_step(moving[:height])]


class Packing:
    def __init__(self, levels, rows, cols, width, n_blk):
        self.levels, self.rows, self.cols, self.width, self.n_blk = levels, rows, cols, width, n_blk
        self.top = (2 ** (levels - 1) - 1) * rows
        self.low = (levels - 1) * (cols + 2 * rows)
        self.fold = width // cols
        self.fits = (
            self.low == width
            and width == n_blk * rows
            and rows % (8 * self.fold) == 0
            and n_blk == 2 ** (n_blk.bit_length() - 1)
        )
        self.height = self.top + rows + rows // self.fold

    def rhs(self, piece, level):
        rows, cols = self.rows, self.cols
        if level < self.levels - 1:
            return piece[self.top : self.top + rows, level * cols : (level + 1) * cols]
        start, step = self.top + rows, rows // self.fold
        return jnp.concatenate(
            [piece[start : start + step, j * cols : (j + 1) * cols] for j in range(self.fold)], axis=0
        )

    def extend(self, piece, level):
        rows = self.rows
        first = (self.levels - 1) * self.cols + level * 2 * rows
        return jnp.concatenate(
            [piece[self.top : self.top + rows, first + h * rows : first + (h + 1) * rows] for h in (0, 1)],
            axis=0,
        )

    def diag(self, pieces, level, diag_ref, first=None):
        first = (2**level - 1) * self.rows if first is None else first
        for m, piece in enumerate(pieces):
            for p in range(2**level):
                diag_ref[block_of(self, m, p), :] = piece[first + p * self.rows : first + (p + 1) * self.rows, :]


def pack_kernel(pk, rhs_hbm, panels_hbm, maps_hbm, diag_hbm, out_ref, last_ref, rhs_ref, panels_ref, maps_ref, sems):
    rows = pk.rows
    pairs = [
        (rhs_hbm, rhs_ref),
        (panels_hbm, panels_ref),
        (maps_hbm, maps_ref),
        (diag_hbm.at[: pk.top], out_ref.at[: pk.top]),
        (diag_hbm.at[pk.top :], last_ref),
    ]
    copies = [pltpu.make_async_copy(a, b, sems.at[i]) for i, (a, b) in enumerate(pairs)]
    for copy in copies:
        copy.start()
    for copy in copies[:3]:
        copy.wait()
    parts = [rhs_ref[l, 0, 0] for l in range(pk.levels - 1)]
    for l in range(pk.levels - 1):
        for h in (0, 1):
            panel = panels_ref[l, 0, 0, h]
            row_ids = lax.broadcasted_iota(jnp.int32, (rows, panel.shape[0]), 0)
            names = maps_ref[l, 0, 0, h : h + 1, :]
            onehot = jnp.where(row_ids == names, 1.0, 0.0).astype(jnp.float32)
            parts.append(dot(onehot, panel))
    out_ref[pk.top : pk.top + rows, :] = jnp.concatenate(parts, axis=1)
    last = rhs_ref[pk.levels - 1, 0, 0]
    step = rows // pk.fold
    out_ref[pk.top + rows :, :] = jnp.concatenate(
        [last[j * step : (j + 1) * step] for j in range(pk.fold)], axis=1
    )
    for copy in copies[3:]:
        copy.wait()


def block_of(pk, m, p=0):
    count = pk.n_blk
    place = ring_place(lax.axis_index("blk"), count)
    turn = ring_offsets(count)[m] * (1 - 2 * (lax.axis_index("cube") % 2))
    group = ring_group((place - turn + count) % count, count)
    return pl.ds(pl.multiple_of(p * pk.width + group * pk.rows, pk.rows), pk.rows)


def extend_out(pk, level, pieces, y_ref, send_ref):
    rows, cols = pk.rows, pk.cols
    for m, piece in enumerate(pieces):
        place = block_of(pk, m)
        e = dot(pk.extend(piece, level), y_ref[place, :])
        send_ref[place, :cols] = pk.rhs(piece, level + 1) - e[:rows]
        send_ref[place, cols:] = e[rows:]


def first_kernel(pk, *refs):
    pieces, (send_ref, y_ref, diag_ref, z_ref) = refs[: pk.n_blk], refs[pk.n_blk :]
    pk.diag(pieces, 0, diag_ref)
    for m, piece in enumerate(pieces):
        z_ref[block_of(pk, m), :] = pk.rhs(piece, 0)
    y_ref[...] = dot_t(diag_ref[...], z_ref[...])
    extend_out(pk, 0, pieces, y_ref, send_ref)


def middle_kernel(pk, *refs):
    pieces, (mine_ref, got_ref, send_ref, y_ref, diag_ref) = refs[: pk.n_blk], refs[pk.n_blk :]
    cols = pk.cols
    own = mine_ref[:, :cols] - got_ref[:, cols:]
    other = got_ref[:, :cols] - mine_ref[:, cols:]
    upper = lax.axis_index("cube") % 2 == 1
    z = jnp.concatenate([jnp.where(upper, other, own), jnp.where(upper, own, other)], axis=0)
    pk.diag(pieces, 1, diag_ref)
    y_ref[...] = dot_t(diag_ref[...], z)
    extend_out(pk, 1, pieces, y_ref, send_ref)


def meet_kernel(pk, mine_ref, got_ref, out_ref):
    cols = pk.cols
    out_ref[:, :cols] = mine_ref[:, :cols] - got_ref[:, cols:]
    out_ref[:, cols:] = got_ref[:, :cols] - mine_ref[:, cols:]


def top_kernel(pk, *refs):
    pieces, (mine_ref, got_ref, keep_ref, send_ref, diag_ref, vec_ref) = refs[: pk.n_blk], refs[pk.n_blk :]
    node, cols = pk.width, pk.cols
    cube = lax.axis_index("cube")

    def part(k):
        return pl.ds(pl.multiple_of((cube ^ k) * node, node), node)

    pk.diag(pieces, 2, diag_ref, 0)
    vec_ref[part(0), :] = mine_ref[:, :cols]
    vec_ref[part(2), :] = mine_ref[:, cols:]
    vec_ref[part(1), :] = got_ref[:, :cols]
    vec_ref[part(3), :] = got_ref[:, cols:]
    diag = diag_ref[...]
    vec_ref[...] = dot(diag, dot_t(diag, vec_ref[...]))
    keep_ref[:, :cols] = vec_ref[part(0), :]
    keep_ref[:, cols:] = vec_ref[part(2), :]
    send_ref[:, :cols] = vec_ref[part(1), :]
    send_ref[:, cols:] = vec_ref[part(3), :]


def turn_kernel(pk, mine_ref, got_ref, held_ref, send_ref):
    cols = pk.cols
    held = mine_ref[...] + got_ref[...]
    held_ref[...] = held
    send_ref[:, :cols] = held[:, cols:]
    send_ref[:, cols:] = held[:, :cols]


def reduce_rows(pk, level, pieces, y_ref, mine_ref, got_ref, w_ref):
    cols = pk.cols
    for m, piece in enumerate(pieces):
        place = block_of(pk, m)
        pair = mine_ref[place, :] + got_ref[place, :]
        both = jnp.concatenate([pair[:, :cols], pair[:, cols:]], axis=0)
        w_ref[place, :] = y_ref[place, :] - dot_t(pk.extend(piece, level), both)


def down_kernel(pk, *refs):
    pieces, refs = refs[: pk.n_blk], refs[pk.n_blk :]
    y_ref, mine_ref, got_ref, keep_ref, send_ref, top_ref, w_ref, diag_ref = refs
    node, cols = pk.width, pk.cols
    own_rows = block_of(pk, 0)
    top_ref[...] = mine_ref[own_rows, :cols] + got_ref[own_rows, :cols]
    pk.diag(pieces, 1, diag_ref)
    reduce_rows(pk, 1, pieces, y_ref, mine_ref, got_ref, w_ref)
    x = dot(diag_ref[...], w_ref[...])
    upper = lax.axis_index("cube") % 2 == 1
    own = jnp.where(upper, x[node:], x[:node])
    other = jnp.where(upper, x[:node], x[node:])
    keep_ref[:, :cols] = own
    keep_ref[:, cols:] = other
    send_ref[:, :cols] = other
    send_ref[:, cols:] = own


def last_kernel(pk, *refs):
    pieces, (y_ref, mine_ref, got_ref, top_ref, out_ref, w_ref) = refs[: pk.n_blk], refs[pk.n_blk :]
    cols = pk.cols
    own_rows = block_of(pk, 0)
    out_ref[2] = top_ref[...]
    out_ref[1] = mine_ref[own_rows, :cols] + got_ref[own_rows, :cols]
    reduce_rows(pk, 0, pieces, y_ref, mine_ref, got_ref, w_ref)
    out_ref[0] = dot(pieces[0][: pk.rows, :], w_ref[...])


def call(kernel, pk, args, outs, scratch=(), place=pltpu.VMEM, room=24):
    vmem = pl.BlockSpec(memory_space=pltpu.VMEM)
    return pl.pallas_call(
        functools.partial(kernel, pk),
        out_shape=[jax.ShapeDtypeStruct(s, jnp.float32) for s in outs],
        in_specs=[pl.BlockSpec(memory_space=place)] * len(args),
        out_specs=[vmem] * len(outs),
        scratch_shapes=scratch,
        compiler_params=pltpu.CompilerParams(vmem_limit_bytes=room * 2**20),
    )(*args)


def tie(value, other):
    return lax.optimization_barrier((value, other))[0]


def gathered(pk, right_side, diag_inverse, panels, extend_map):
    rows, cols, node = pk.rows, pk.cols, pk.width
    one, two = (node, cols), (node, 2 * cols)

    def work(*shapes):
        return [pltpu.VMEM(s, jnp.float32) for s in shapes]

    inputs = [right_side, panels, extend_map, diag_inverse]
    packed, top = call(
        pack_kernel,
        pk,
        inputs,
        [(pk.height, node), (diag_inverse.shape[0] - pk.top, node)],
        [pltpu.VMEM(a.shape, a.dtype) for a in inputs[:3]] + [pltpu.SemaphoreType.DMA((5,))],
        pltpu.HBM,
        60,
    )
    first = gather_rows(packed)
    last = gather_rows(top)
    send, y0 = call(first_kernel, pk, first, [two, one], work((node, node), one))
    got = swap(send, "cube", 1)
    send, y1 = call(middle_kernel, pk, [*first, send, got], [two, one], work((2 * node, node)))
    got = swap(send, "cube", 2)
    (held,) = call(meet_kernel, pk, [send, got], [two])
    got = swap(held, "cube", 1)
    keep, send = call(
        top_kernel, pk, [*last, held, got], [two, two], work((4 * node, node), (4 * node, cols))
    )
    held, send = call(turn_kernel, pk, [keep, swap(send, "cube", 1)], [two, two])
    got = swap(send, "cube", 2)
    keep, send, top = call(
        down_kernel, pk, [*first, y1, held, got], [two, two, (rows, cols)], work(one, (2 * node, node))
    )
    got = swap(send, "cube", 1)
    (out,) = call(last_kernel, pk, [*first, y0, keep, got, top], [(3, rows, cols)], work(one))
    return out[:, None, None]


def from_partner(block, axis, apart):
    count = lax.axis_size(axis)
    route = []
    for low in range(count):
        high = low | 1 << apart
        if high != low and high < count:
            route += [(low, high), (high, low)]
    return lax.ppermute(block, axis, route)


def collect_pairs(residual_rows, tree_level, cube_index):
    gathered = residual_rows
    for bit_index in range(tree_level):
        partner_rows = from_partner(gathered, "cube", bit_index)
        lower_side = cube_index // 2**bit_index % 2 == 0
        gathered = jnp.where(
            lower_side,
            jnp.concatenate([gathered, partner_rows], axis=0),
            jnp.concatenate([partner_rows, gathered], axis=0),
        )
    return gathered


def reduce_pairs(partial_value, tree_level, cube_index):
    for bit_index in reversed(range(tree_level)):
        half_rows = partial_value.shape[0] // 2
        lower_rows = partial_value[:half_rows]
        upper_rows = partial_value[half_rows:]
        lower_side = cube_index // 2**bit_index % 2 == 0
        kept_rows = jnp.where(lower_side, lower_rows, upper_rows)
        sent_rows = jnp.where(lower_side, upper_rows, lower_rows)
        partial_value = kept_rows + from_partner(sent_rows, "cube", bit_index)
    return partial_value


def stepwise(right_side, diag_inverse, panels, extend_map):
    highest = lax.Precision.HIGHEST
    levels = right_side.shape[0]
    local_rows = right_side.shape[3]
    columns_k = right_side.shape[4]
    cube_index = lax.axis_index("cube")
    rhs_rows = right_side[:, 0, 0]
    panel_blocks = panels[:, 0, 0]
    row_maps = extend_map[:, 0, 0]
    row_ids = jnp.arange(local_rows, dtype=jnp.int32)
    update = jnp.zeros((local_rows, columns_k), jnp.float32)
    solved = []
    onehots = []
    diag_blocks = []
    for tree_level in range(levels):
        span_rows = 2**tree_level * local_rows
        offset = (2**tree_level - 1) * local_rows
        diag_block = diag_inverse[offset : offset + span_rows]
        diag_blocks.append(diag_block)
        residual_rows = rhs_rows[tree_level] - update
        column = collect_pairs(residual_rows, tree_level, cube_index)

        def term_rows(first_row, row_count, diag_block=diag_block, column=column):
            return jnp.einsum("ir,ik->rk", diag_block, column, precision=highest)

        solved_rows = lax.psum_scatter(
            term_rows(jnp.int32(0), lax.axis_size("blk") * local_rows),
            "blk",
            scatter_dimension=0,
            tiled=True,
        )
        solved.append(solved_rows)
        if tree_level + 1 < levels:
            onehot = (row_maps[tree_level][..., None] == row_ids).astype(jnp.float32)
            onehots.append(onehot)
            upd_rows = jnp.einsum(
                "hmr,rk->hmk", panel_blocks[tree_level], solved_rows, precision=highest
            )
            extended = jnp.einsum("hmt,hmk->htk", onehot, upd_rows, precision=highest)
            update = extended[0] + from_partner(extended[1], "cube", tree_level)
    results = [None] * levels
    parent = None
    for tree_level in reversed(range(levels)):
        span_rows = 2**tree_level * local_rows
        diag_block = diag_blocks[tree_level]
        work_rows = solved[tree_level]
        if parent is not None:
            partner_rows = from_partner(parent, "cube", tree_level)
            parent_pair = jnp.stack([parent, partner_rows], axis=0)
            fetched = jnp.einsum(
                "hmt,htk->hmk", onehots[tree_level], parent_pair, precision=highest
            )
            work_rows = work_rows - jnp.einsum(
                "hmr,hmk->rk", panel_blocks[tree_level], fetched, precision=highest
            )

        def accumulate(running, shard_rows, first_row, diag_block=diag_block):
            return jnp.einsum("ir,rk->ik", diag_block, shard_rows, precision=highest)

        initial = jnp.zeros((span_rows, columns_k), jnp.float32)
        partial_value = accumulate(
            initial, lax.all_gather(work_rows, "blk", axis=0, tiled=True), jnp.int32(0)
        )
        parent = reduce_pairs(partial_value, tree_level, cube_index)
        results[tree_level] = parent
    return jnp.stack(results)[:, None, None]

def body(right_side, diag_inverse, panels, extend_map):
    levels, _, _, rows, cols = right_side.shape
    n_blk = lax.axis_size("blk")
    pk = Packing(levels, rows, cols, diag_inverse.shape[1], n_blk)
    small = n_blk * diag_inverse.size * 4 <= GATHER_BYTES
    if levels == 3 and lax.axis_size("cube") == 4 and pk.fits and small:
        return gathered(pk, right_side, diag_inverse, panels, extend_map)
    return stepwise(right_side, diag_inverse, panels, extend_map)


def solution(mesh):
    placed = (
        P(None, "cube", "blk", None, None),
        P("cube", "blk"),
        P(None, "cube", "blk", None, None, None),
        P(None, "cube", "blk", None, None),
    )
    return jax.shard_map(
        body,
        mesh=mesh,
        in_specs=placed,
        out_specs=P(None, "cube", "blk", None, None),
        check_vma=False,
    )
```

```python
import functools

import jax
import jax.numpy as jnp
from jax import lax
from jax.experimental import pallas as pl
from jax.experimental.pallas import tpu as pltpu
from jax.sharding import PartitionSpec as P

GATHER_BYTES = 8 * 2**20


def split(a):
    high = a.astype(jnp.bfloat16)
    return high, (a - high.astype(jnp.float32)).astype(jnp.bfloat16)


def product(a, b, dims):
    def term(x, y):
        return lax.dot_general(x, y, (dims, ((), ())), preferred_element_type=jnp.float32)

    (a_high, a_low), (b_high, b_low) = a, b
    return term(a_high, b_high) + (term(a_high, b_low) + term(a_low, b_high))


def dot(a, b):
    return product(split(a), split(b), ((1,), (0,)))


def dot_t(a, b):
    return product(split(a), split(b), ((0,), (0,)))


def swap(block, axis, mask):
    count = lax.axis_size(axis)
    return lax.ppermute(block, axis, [(i, i ^ mask) for i in range(count)])


def ring_place(blk, count):
    return jnp.where(blk % 2 == 0, blk // 2, count - 1 - blk // 2)


def ring_group(place, count):
    return jnp.where(place < count // 2, 2 * place, 2 * (count - 1 - place) + 1)


def ring_step(block):
    cubes, count = lax.axis_size("cube"), lax.axis_size("blk")
    order = list(range(0, count, 2)) + list(range(count - 1, 0, -2))
    route = [
        (c * count + order[i], c * count + order[(i + 1 - 2 * (c % 2)) % count])
        for c in range(cubes)
        for i in range(count)
    ]
    return lax.ppermute(block, ("cube", "blk"), route)


def ring_offsets(count):
    return [0] + [x for r in range(1, count // 2) for x in (r, -r)] + [count // 2]


def gather_rows(block):
    height = block.shape[0]
    moving = jnp.concatenate([block, swap(block, "cube", 1)], axis=0)
    out = [block]
    for _ in range(1, lax.axis_size("blk") // 2):
        moving = ring_step(moving)
        out += [moving[:height], swap(moving[height:], "cube", 1)]
    return out + [ring_step(moving[:height])]


class Packing:
    def __init__(self, levels, rows, cols, width, n_blk):
        self.levels, self.rows, self.cols, self.width, self.n_blk = levels, rows, cols, width, n_blk
        self.top = (2 ** (levels - 1) - 1) * rows
        self.low = (levels - 1) * (cols + 2 * rows)
        self.fold = width // cols
        self.fits = (
            self.low == width
            and width == n_blk * rows
            and rows % (8 * self.fold) == 0
            and n_blk == 2 ** (n_blk.bit_length() - 1)
        )
        self.height = self.top + rows + rows // self.fold

    def rhs(self, piece, level):
        rows, cols = self.rows, self.cols
        if level < self.levels - 1:
            return piece[self.top : self.top + rows, level * cols : (level + 1) * cols]
        start, step = self.top + rows, rows // self.fold
        return jnp.concatenate(
            [piece[start : start + step, j * cols : (j + 1) * cols] for j in range(self.fold)], axis=0
        )

    def extend(self, piece, level):
        rows = self.rows
        first = (self.levels - 1) * self.cols + level * 2 * rows
        return jnp.concatenate(
            [piece[self.top : self.top + rows, first + h * rows : first + (h + 1) * rows] for h in (0, 1)],
            axis=0,
        )

    def diag(self, pieces, level, diag_ref, first=None):
        first = (2**level - 1) * self.rows if first is None else first
        for m, piece in enumerate(pieces):
            for p in range(2**level):
                diag_ref[block_of(self, m, p), :] = piece[first + p * self.rows : first + (p + 1) * self.rows, :]


def pack_kernel(pk, rhs_hbm, panels_hbm, maps_hbm, diag_hbm, out_ref, last_ref, rhs_ref, panels_ref, maps_ref, sems):
    rows = pk.rows
    pairs = [
        (rhs_hbm, rhs_ref),
        (panels_hbm, panels_ref),
        (maps_hbm, maps_ref),
        (diag_hbm.at[: pk.top], out_ref.at[: pk.top]),
        (diag_hbm.at[pk.top :], last_ref),
    ]
    copies = [pltpu.make_async_copy(a, b, sems.at[i]) for i, (a, b) in enumerate(pairs)]
    for copy in copies:
        copy.start()
    for copy in copies[:3]:
        copy.wait()
    parts = [rhs_ref[l, 0, 0] for l in range(pk.levels - 1)]
    for l in range(pk.levels - 1):
        for h in (0, 1):
            panel = panels_ref[l, 0, 0, h]
            row_ids = lax.broadcasted_iota(jnp.int32, (rows, panel.shape[0]), 0)
            names = maps_ref[l, 0, 0, h : h + 1, :]
            onehot = jnp.where(row_ids == names, 1.0, 0.0).astype(jnp.float32)
            parts.append(
                jnp.dot(onehot, panel, precision=lax.Precision.HIGHEST, preferred_element_type=jnp.float32)
            )
    out_ref[pk.top : pk.top + rows, :] = jnp.concatenate(parts, axis=1)
    last = rhs_ref[pk.levels - 1, 0, 0]
    step = rows // pk.fold
    out_ref[pk.top + rows :, :] = jnp.concatenate(
        [last[j * step : (j + 1) * step] for j in range(pk.fold)], axis=1
    )
    for copy in copies[3:]:
        copy.wait()


def block_of(pk, m, p=0):
    count = pk.n_blk
    place = ring_place(lax.axis_index("blk"), count)
    turn = ring_offsets(count)[m] * (1 - 2 * (lax.axis_index("cube") % 2))
    group = ring_group((place - turn + count) % count, count)
    return pl.ds(pl.multiple_of(p * pk.width + group * pk.rows, pk.rows), pk.rows)


def extend_out(pk, level, pieces, y_ref, send_ref):
    rows, cols = pk.rows, pk.cols
    for m, piece in enumerate(pieces):
        place = block_of(pk, m)
        e = dot(pk.extend(piece, level), y_ref[place, :])
        send_ref[place, :cols] = pk.rhs(piece, level + 1) - e[:rows]
        send_ref[place, cols:] = e[rows:]


def first_kernel(pk, *refs):
    pieces, (send_ref, y_ref, diag_ref, z_ref) = refs[: pk.n_blk], refs[pk.n_blk :]
    pk.diag(pieces, 0, diag_ref)
    for m, piece in enumerate(pieces):
        z_ref[block_of(pk, m), :] = pk.rhs(piece, 0)
    y_ref[...] = dot_t(diag_ref[...], z_ref[...])
    extend_out(pk, 0, pieces, y_ref, send_ref)


def middle_kernel(pk, *refs):
    pieces, (mine_ref, got_ref, send_ref, y_ref, diag_ref) = refs[: pk.n_blk], refs[pk.n_blk :]
    cols = pk.cols
    own = mine_ref[:, :cols] - got_ref[:, cols:]
    other = got_ref[:, :cols] - mine_ref[:, cols:]
    upper = lax.axis_index("cube") % 2 == 1
    z = jnp.concatenate([jnp.where(upper, other, own), jnp.where(upper, own, other)], axis=0)
    pk.diag(pieces, 1, diag_ref)
    y_ref[...] = dot_t(diag_ref[...], z)
    extend_out(pk, 1, pieces, y_ref, send_ref)


def meet_kernel(pk, mine_ref, got_ref, out_ref):
    cols = pk.cols
    out_ref[:, :cols] = mine_ref[:, :cols] - got_ref[:, cols:]
    out_ref[:, cols:] = got_ref[:, :cols] - mine_ref[:, cols:]


def top_kernel(pk, *refs):
    pieces, (mine_ref, got_ref, keep_ref, send_ref, diag_ref, vec_ref) = refs[: pk.n_blk], refs[pk.n_blk :]
    node, cols = pk.width, pk.cols
    cube = lax.axis_index("cube")

    def part(k):
        return pl.ds(pl.multiple_of((cube ^ k) * node, node), node)

    pk.diag(pieces, 2, diag_ref, 0)
    vec_ref[part(0), :] = mine_ref[:, :cols]
    vec_ref[part(2), :] = mine_ref[:, cols:]
    vec_ref[part(1), :] = got_ref[:, :cols]
    vec_ref[part(3), :] = got_ref[:, cols:]
    diag = split(diag_ref[...])
    y = product(diag, split(vec_ref[...]), ((0,), (0,)))
    vec_ref[...] = product(diag, split(y), ((1,), (0,)))
    keep_ref[:, :cols] = vec_ref[part(0), :]
    keep_ref[:, cols:] = vec_ref[part(2), :]
    send_ref[:, :cols] = vec_ref[part(1), :]
    send_ref[:, cols:] = vec_ref[part(3), :]


def turn_kernel(pk, mine_ref, got_ref, held_ref, send_ref):
    cols = pk.cols
    held = mine_ref[...] + got_ref[...]
    held_ref[...] = held
    send_ref[:, :cols] = held[:, cols:]
    send_ref[:, cols:] = held[:, :cols]


def reduce_rows(pk, level, pieces, y_ref, mine_ref, got_ref, w_ref):
    cols = pk.cols
    for m, piece in enumerate(pieces):
        place = block_of(pk, m)
        pair = mine_ref[place, :] + got_ref[place, :]
        both = jnp.concatenate([pair[:, :cols], pair[:, cols:]], axis=0)
        w_ref[place, :] = y_ref[place, :] - dot_t(pk.extend(piece, level), both)


def down_kernel(pk, *refs):
    pieces, refs = refs[: pk.n_blk], refs[pk.n_blk :]
    y_ref, mine_ref, got_ref, keep_ref, send_ref, top_ref, w_ref, diag_ref = refs
    node, cols = pk.width, pk.cols
    own_rows = block_of(pk, 0)
    top_ref[...] = mine_ref[own_rows, :cols] + got_ref[own_rows, :cols]
    pk.diag(pieces, 1, diag_ref)
    reduce_rows(pk, 1, pieces, y_ref, mine_ref, got_ref, w_ref)
    x = dot(diag_ref[...], w_ref[...])
    upper = lax.axis_index("cube") % 2 == 1
    own = jnp.where(upper, x[node:], x[:node])
    other = jnp.where(upper, x[:node], x[node:])
    keep_ref[:, :cols] = own
    keep_ref[:, cols:] = other
    send_ref[:, :cols] = other
    send_ref[:, cols:] = own


def last_kernel(pk, *refs):
    pieces, (y_ref, mine_ref, got_ref, top_ref, out_ref, w_ref) = refs[: pk.n_blk], refs[pk.n_blk :]
    cols = pk.cols
    own_rows = block_of(pk, 0)
    out_ref[2] = top_ref[...]
    out_ref[1] = mine_ref[own_rows, :cols] + got_ref[own_rows, :cols]
    reduce_rows(pk, 0, pieces, y_ref, mine_ref, got_ref, w_ref)
    out_ref[0] = dot(pieces[0][: pk.rows, :], w_ref[...])


def call(kernel, pk, args, outs, scratch=(), place=pltpu.VMEM, room=24):
    vmem = pl.BlockSpec(memory_space=pltpu.VMEM)
    return pl.pallas_call(
        functools.partial(kernel, pk),
        out_shape=[jax.ShapeDtypeStruct(s, jnp.float32) for s in outs],
        in_specs=[pl.BlockSpec(memory_space=place)] * len(args),
        out_specs=[vmem] * len(outs),
        scratch_shapes=scratch,
        compiler_params=pltpu.CompilerParams(vmem_limit_bytes=room * 2**20),
    )(*args)


def tie(value, other):
    return lax.optimization_barrier((value, other))[0]


def gathered(pk, right_side, diag_inverse, panels, extend_map):
    rows, cols, node = pk.rows, pk.cols, pk.width
    one, two = (node, cols), (node, 2 * cols)

    def work(*shapes):
        return [pltpu.VMEM(s, jnp.float32) for s in shapes]

    inputs = [right_side, panels, extend_map, diag_inverse]
    packed, top = call(
        pack_kernel,
        pk,
        inputs,
        [(pk.height, node), (diag_inverse.shape[0] - pk.top, node)],
        [pltpu.VMEM(a.shape, a.dtype) for a in inputs[:3]] + [pltpu.SemaphoreType.DMA((5,))],
        pltpu.HBM,
        60,
    )
    first = gather_rows(packed)
    last = gather_rows(top)
    send, y0 = call(first_kernel, pk, first, [two, one], work((node, node), one))
    got = swap(send, "cube", 1)
    send, y1 = call(middle_kernel, pk, [*first, send, got], [two, one], work((2 * node, node)))
    got = swap(send, "cube", 2)
    (held,) = call(meet_kernel, pk, [send, got], [two])
    got = swap(held, "cube", 1)
    keep, send = call(
        top_kernel, pk, [*last, held, got], [two, two], work((4 * node, node), (4 * node, cols))
    )
    held, send = call(turn_kernel, pk, [keep, swap(send, "cube", 1)], [two, two])
    got = swap(send, "cube", 2)
    keep, send, top = call(
        down_kernel, pk, [*first, y1, held, got], [two, two, (rows, cols)], work(one, (2 * node, node))
    )
    got = swap(send, "cube", 1)
    (out,) = call(last_kernel, pk, [*first, y0, keep, got, top], [(3, rows, cols)], work(one))
    return out[:, None, None]


def from_partner(block, axis, apart):
    count = lax.axis_size(axis)
    route = []
    for low in range(count):
        high = low | 1 << apart
        if high != low and high < count:
            route += [(low, high), (high, low)]
    return lax.ppermute(block, axis, route)


def collect_pairs(residual_rows, tree_level, cube_index):
    gathered = residual_rows
    for bit_index in range(tree_level):
        partner_rows = from_partner(gathered, "cube", bit_index)
        lower_side = cube_index // 2**bit_index % 2 == 0
        gathered = jnp.where(
            lower_side,
            jnp.concatenate([gathered, partner_rows], axis=0),
            jnp.concatenate([partner_rows, gathered], axis=0),
        )
    return gathered


def reduce_pairs(partial_value, tree_level, cube_index):
    for bit_index in reversed(range(tree_level)):
        half_rows = partial_value.shape[0] // 2
        lower_rows = partial_value[:half_rows]
        upper_rows = partial_value[half_rows:]
        lower_side = cube_index // 2**bit_index % 2 == 0
        kept_rows = jnp.where(lower_side, lower_rows, upper_rows)
        sent_rows = jnp.where(lower_side, upper_rows, lower_rows)
        partial_value = kept_rows + from_partner(sent_rows, "cube", bit_index)
    return partial_value


def stepwise(right_side, diag_inverse, panels, extend_map):
    highest = lax.Precision.HIGHEST
    levels = right_side.shape[0]
    local_rows = right_side.shape[3]
    columns_k = right_side.shape[4]
    cube_index = lax.axis_index("cube")
    rhs_rows = right_side[:, 0, 0]
    panel_blocks = panels[:, 0, 0]
    row_maps = extend_map[:, 0, 0]
    row_ids = jnp.arange(local_rows, dtype=jnp.int32)
    update = jnp.zeros((local_rows, columns_k), jnp.float32)
    solved = []
    onehots = []
    diag_blocks = []
    for tree_level in range(levels):
        span_rows = 2**tree_level * local_rows
        offset = (2**tree_level - 1) * local_rows
        diag_block = diag_inverse[offset : offset + span_rows]
        diag_blocks.append(diag_block)
        residual_rows = rhs_rows[tree_level] - update
        column = collect_pairs(residual_rows, tree_level, cube_index)

        def term_rows(first_row, row_count, diag_block=diag_block, column=column):
            return jnp.einsum("ir,ik->rk", diag_block, column, precision=highest)

        solved_rows = lax.psum_scatter(
            term_rows(jnp.int32(0), lax.axis_size("blk") * local_rows),
            "blk",
            scatter_dimension=0,
            tiled=True,
        )
        solved.append(solved_rows)
        if tree_level + 1 < levels:
            onehot = (row_maps[tree_level][..., None] == row_ids).astype(jnp.float32)
            onehots.append(onehot)
            upd_rows = jnp.einsum(
                "hmr,rk->hmk", panel_blocks[tree_level], solved_rows, precision=highest
            )
            extended = jnp.einsum("hmt,hmk->htk", onehot, upd_rows, precision=highest)
            update = extended[0] + from_partner(extended[1], "cube", tree_level)
    results = [None] * levels
    parent = None
    for tree_level in reversed(range(levels)):
        span_rows = 2**tree_level * local_rows
        diag_block = diag_blocks[tree_level]
        work_rows = solved[tree_level]
        if parent is not None:
            partner_rows = from_partner(parent, "cube", tree_level)
            parent_pair = jnp.stack([parent, partner_rows], axis=0)
            fetched = jnp.einsum(
                "hmt,htk->hmk", onehots[tree_level], parent_pair, precision=highest
            )
            work_rows = work_rows - jnp.einsum(
                "hmr,hmk->rk", panel_blocks[tree_level], fetched, precision=highest
            )

        def accumulate(running, shard_rows, first_row, diag_block=diag_block):
            return jnp.einsum("ir,rk->ik", diag_block, shard_rows, precision=highest)

        initial = jnp.zeros((span_rows, columns_k), jnp.float32)
        partial_value = accumulate(
            initial, lax.all_gather(work_rows, "blk", axis=0, tiled=True), jnp.int32(0)
        )
        parent = reduce_pairs(partial_value, tree_level, cube_index)
        results[tree_level] = parent
    return jnp.stack(results)[:, None, None]

def body(right_side, diag_inverse, panels, extend_map):
    levels, _, _, rows, cols = right_side.shape
    n_blk = lax.axis_size("blk")
    pk = Packing(levels, rows, cols, diag_inverse.shape[1], n_blk)
    small = n_blk * diag_inverse.size * 4 <= GATHER_BYTES
    if levels == 3 and lax.axis_size("cube") == 4 and pk.fits and small:
        return gathered(pk, right_side, diag_inverse, panels, extend_map)
    return stepwise(right_side, diag_inverse, panels, extend_map)


def solution(mesh):
    placed = (
        P(None, "cube", "blk", None, None),
        P("cube", "blk"),
        P(None, "cube", "blk", None, None, None),
        P(None, "cube", "blk", None, None),
    )
    return jax.shard_map(
        body,
        mesh=mesh,
        in_specs=placed,
        out_specs=P(None, "cube", "blk", None, None),
        check_vma=False,
    )
```

```python
import functools

import jax
import jax.numpy as jnp
from jax import lax
from jax.experimental import pallas as pl
from jax.experimental.pallas import tpu as pltpu
from jax.sharding import PartitionSpec as P

GATHER_BYTES = 8 * 2**20


def split(a):
    high = a.astype(jnp.bfloat16)
    return high, (a - high.astype(jnp.float32)).astype(jnp.bfloat16)


def product(a, b, dims):
    def term(x, y):
        return lax.dot_general(x, y, (dims, ((), ())), preferred_element_type=jnp.float32)

    (a_high, a_low), (b_high, b_low) = a, b
    return term(a_high, b_high) + (term(a_high, b_low) + term(a_low, b_high))


def dot(a, b):
    return product(split(a), split(b), ((1,), (0,)))


def dot_t(a, b):
    return product(split(a), split(b), ((0,), (0,)))


def swap(block, axis, mask):
    count = lax.axis_size(axis)
    return lax.ppermute(block, axis, [(i, i ^ mask) for i in range(count)])


def ring_place(blk, count):
    return jnp.where(blk % 2 == 0, blk // 2, count - 1 - blk // 2)


def ring_group(place, count):
    return jnp.where(place < count // 2, 2 * place, 2 * (count - 1 - place) + 1)


def ring_step(block, even, odd):
    cubes, count = lax.axis_size("cube"), lax.axis_size("blk")
    order = list(range(0, count, 2)) + list(range(count - 1, 0, -2))
    route = [
        (c * count + order[i], c * count + order[(i + (odd if c % 2 else even)) % count])
        for c in range(cubes)
        for i in range(count)
    ]
    return lax.ppermute(block, ("cube", "blk"), route)


def ring_offsets(count):
    return [0] + [x for r in range(1, count // 2) for x in (r, -r)] + [count // 2]


def gather_rows(block):
    height = block.shape[0]
    moving = jnp.concatenate([block, swap(block, "cube", 1)], axis=0)
    out = [block]
    for _ in range(1, lax.axis_size("blk") // 2):
        moving = ring_step(moving, 1, -1)
        out += [moving[:height], swap(moving[height:], "cube", 1)]
    return out + [ring_step(moving[:height], 1, -1)]


def gather_both_ways(block):
    out = [block]
    up = down = block
    for _ in range(1, lax.axis_size("blk") // 2):
        up, down = ring_step(up, 1, 1), ring_step(down, -1, -1)
        out += [up, down]
    return out + [ring_step(up, 1, 1)]


class Packing:
    def __init__(self, levels, rows, cols, width, n_blk):
        self.levels, self.rows, self.cols, self.width, self.n_blk = levels, rows, cols, width, n_blk
        self.top = (2 ** (levels - 1) - 1) * rows
        self.low = (levels - 1) * (cols + 2 * rows)
        self.fold = width // cols
        self.fits = (
            self.low == width
            and width == n_blk * rows
            and rows % (8 * self.fold) == 0
            and n_blk == 2 ** (n_blk.bit_length() - 1)
        )
        self.height = self.top + rows + rows // self.fold

    def rhs(self, piece, level):
        rows, cols = self.rows, self.cols
        if level < self.levels - 1:
            return piece[self.top : self.top + rows, level * cols : (level + 1) * cols]
        start, step = self.top + rows, rows // self.fold
        return jnp.concatenate(
            [piece[start : start + step, j * cols : (j + 1) * cols] for j in range(self.fold)], axis=0
        )

    def extend(self, piece, level):
        rows = self.rows
        first = (self.levels - 1) * self.cols + level * 2 * rows
        return jnp.concatenate(
            [piece[self.top : self.top + rows, first + h * rows : first + (h + 1) * rows] for h in (0, 1)],
            axis=0,
        )

    def diag(self, pieces, level, diag_ref, place_of, first=None):
        first = (2**level - 1) * self.rows if first is None else first
        for m, piece in enumerate(pieces):
            for p in range(2**level):
                diag_ref[place_of(self, m, p), :] = piece[first + p * self.rows : first + (p + 1) * self.rows, :]


def pack_kernel(pk, rhs_hbm, panels_hbm, maps_hbm, diag_hbm, out_ref, last_ref, rhs_ref, panels_ref, maps_ref, sems):
    rows = pk.rows
    pairs = [
        (rhs_hbm, rhs_ref),
        (panels_hbm, panels_ref),
        (maps_hbm, maps_ref),
        (diag_hbm.at[: pk.top], out_ref.at[: pk.top]),
        (diag_hbm.at[pk.top :], last_ref),
    ]
    copies = [pltpu.make_async_copy(a, b, sems.at[i]) for i, (a, b) in enumerate(pairs)]
    for copy in copies:
        copy.start()
    for copy in copies[:3]:
        copy.wait()
    parts = [rhs_ref[l, 0, 0] for l in range(pk.levels - 1)]
    for l in range(pk.levels - 1):
        for h in (0, 1):
            panel = panels_ref[l, 0, 0, h]
            row_ids = lax.broadcasted_iota(jnp.int32, (rows, panel.shape[0]), 0)
            names = maps_ref[l, 0, 0, h : h + 1, :]
            onehot = jnp.where(row_ids == names, 1.0, 0.0).astype(jnp.float32)
            parts.append(
                jnp.dot(onehot, panel, precision=lax.Precision.HIGHEST, preferred_element_type=jnp.float32)
            )
    out_ref[pk.top : pk.top + rows, :] = jnp.concatenate(parts, axis=1)
    last = rhs_ref[pk.levels - 1, 0, 0]
    step = rows // pk.fold
    out_ref[pk.top + rows :, :] = jnp.concatenate(
        [last[j * step : (j + 1) * step] for j in range(pk.fold)], axis=1
    )
    for copy in copies[3:]:
        copy.wait()


def block_of(pk, m, p=0, side=1):
    count = pk.n_blk
    place = ring_place(lax.axis_index("blk"), count)
    group = ring_group((place - ring_offsets(count)[m] * side + count) % count, count)
    return pl.ds(pl.multiple_of(p * pk.width + group * pk.rows, pk.rows), pk.rows)


def shared_block_of(pk, m, p=0):
    return block_of(pk, m, p, 1 - 2 * (lax.axis_index("cube") % 2))


def extend_out(pk, level, pieces, y_ref, send_ref):
    rows, cols = pk.rows, pk.cols
    for m, piece in enumerate(pieces):
        place = block_of(pk, m)
        e = dot(pk.extend(piece, level), y_ref[place, :])
        send_ref[place, :cols] = pk.rhs(piece, level + 1) - e[:rows]
        send_ref[place, cols:] = e[rows:]


def first_kernel(pk, *refs):
    pieces, (send_ref, y_ref, diag_ref, z_ref) = refs[: pk.n_blk], refs[pk.n_blk :]
    pk.diag(pieces, 0, diag_ref, block_of)
    for m, piece in enumerate(pieces):
        z_ref[block_of(pk, m), :] = pk.rhs(piece, 0)
    y_ref[...] = dot_t(diag_ref[...], z_ref[...])
    extend_out(pk, 0, pieces, y_ref, send_ref)


def middle_kernel(pk, *refs):
    pieces, (mine_ref, got_ref, send_ref, y_ref, diag_ref) = refs[: pk.n_blk], refs[pk.n_blk :]
    cols = pk.cols
    own = mine_ref[:, :cols] - got_ref[:, cols:]
    other = got_ref[:, :cols] - mine_ref[:, cols:]
    upper = lax.axis_index("cube") % 2 == 1
    z = jnp.concatenate([jnp.where(upper, other, own), jnp.where(upper, own, other)], axis=0)
    pk.diag(pieces, 1, diag_ref, block_of)
    y_ref[...] = dot_t(diag_ref[...], z)
    extend_out(pk, 1, pieces, y_ref, send_ref)


def meet_kernel(pk, mine_ref, got_ref, out_ref):
    cols = pk.cols
    out_ref[:, :cols] = mine_ref[:, :cols] - got_ref[:, cols:]
    out_ref[:, cols:] = got_ref[:, :cols] - mine_ref[:, cols:]


def top_kernel(pk, *refs):
    pieces, (mine_ref, got_ref, keep_ref, send_ref, diag_ref, vec_ref) = refs[: pk.n_blk], refs[pk.n_blk :]
    node, cols = pk.width, pk.cols
    cube = lax.axis_index("cube")

    def part(k):
        return pl.ds(pl.multiple_of((cube ^ k) * node, node), node)

    pk.diag(pieces, 2, diag_ref, shared_block_of, 0)
    vec_ref[part(0), :] = mine_ref[:, :cols]
    vec_ref[part(2), :] = mine_ref[:, cols:]
    vec_ref[part(1), :] = got_ref[:, :cols]
    vec_ref[part(3), :] = got_ref[:, cols:]
    diag = split(diag_ref[...])
    y = product(diag, split(vec_ref[...]), ((0,), (0,)))
    vec_ref[...] = product(diag, split(y), ((1,), (0,)))
    keep_ref[:, :cols] = vec_ref[part(0), :]
    keep_ref[:, cols:] = vec_ref[part(2), :]
    send_ref[:, :cols] = vec_ref[part(1), :]
    send_ref[:, cols:] = vec_ref[part(3), :]


def turn_kernel(pk, mine_ref, got_ref, held_ref, send_ref):
    cols = pk.cols
    held = mine_ref[...] + got_ref[...]
    held_ref[...] = held
    send_ref[:, :cols] = held[:, cols:]
    send_ref[:, cols:] = held[:, :cols]


def reduce_rows(pk, level, pieces, y_ref, mine_ref, got_ref, w_ref):
    cols = pk.cols
    for m, piece in enumerate(pieces):
        place = block_of(pk, m)
        pair = mine_ref[place, :] + got_ref[place, :]
        both = jnp.concatenate([pair[:, :cols], pair[:, cols:]], axis=0)
        w_ref[place, :] = y_ref[place, :] - dot_t(pk.extend(piece, level), both)


def down_kernel(pk, *refs):
    pieces, refs = refs[: pk.n_blk], refs[pk.n_blk :]
    y_ref, mine_ref, got_ref, keep_ref, send_ref, top_ref, w_ref, diag_ref = refs
    node, cols = pk.width, pk.cols
    own_rows = block_of(pk, 0)
    top_ref[...] = mine_ref[own_rows, :cols] + got_ref[own_rows, :cols]
    pk.diag(pieces, 1, diag_ref, block_of)
    reduce_rows(pk, 1, pieces, y_ref, mine_ref, got_ref, w_ref)
    x = dot(diag_ref[...], w_ref[...])
    upper = lax.axis_index("cube") % 2 == 1
    own = jnp.where(upper, x[node:], x[:node])
    other = jnp.where(upper, x[:node], x[node:])
    keep_ref[:, :cols] = own
    keep_ref[:, cols:] = other
    send_ref[:, :cols] = other
    send_ref[:, cols:] = own


def last_kernel(pk, *refs):
    pieces, (y_ref, mine_ref, got_ref, top_ref, out_ref, w_ref) = refs[: pk.n_blk], refs[pk.n_blk :]
    cols = pk.cols
    own_rows = block_of(pk, 0)
    out_ref[2] = top_ref[...]
    out_ref[1] = mine_ref[own_rows, :cols] + got_ref[own_rows, :cols]
    reduce_rows(pk, 0, pieces, y_ref, mine_ref, got_ref, w_ref)
    out_ref[0] = dot(pieces[0][: pk.rows, :], w_ref[...])


def call(kernel, pk, args, outs, scratch=(), place=pltpu.VMEM, room=24):
    vmem = pl.BlockSpec(memory_space=pltpu.VMEM)
    return pl.pallas_call(
        functools.partial(kernel, pk),
        out_shape=[jax.ShapeDtypeStruct(s, jnp.float32) for s in outs],
        in_specs=[pl.BlockSpec(memory_space=place)] * len(args),
        out_specs=[vmem] * len(outs),
        scratch_shapes=scratch,
        compiler_params=pltpu.CompilerParams(vmem_limit_bytes=room * 2**20),
    )(*args)


def tie(value, other):
    return lax.optimization_barrier((value, other))[0]


def gathered(pk, right_side, diag_inverse, panels, extend_map):
    rows, cols, node = pk.rows, pk.cols, pk.width
    one, two = (node, cols), (node, 2 * cols)

    def work(*shapes):
        return [pltpu.VMEM(s, jnp.float32) for s in shapes]

    inputs = [right_side, panels, extend_map, diag_inverse]
    packed, top = call(
        pack_kernel,
        pk,
        inputs,
        [(pk.height, node), (diag_inverse.shape[0] - pk.top, node)],
        [pltpu.VMEM(a.shape, a.dtype) for a in inputs[:3]] + [pltpu.SemaphoreType.DMA((5,))],
        pltpu.HBM,
        60,
    )
    first = gather_both_ways(packed)
    last = gather_rows(top)
    send, y0 = call(first_kernel, pk, first, [two, one], work((node, node), one))
    got = swap(send, "cube", 1)
    send, y1 = call(middle_kernel, pk, [*first, send, got], [two, one], work((2 * node, node)))
    got = tie(swap(send, "cube", 2), last[7])
    (held,) = call(meet_kernel, pk, [send, got], [two])
    got = swap(held, "cube", 1)
    keep, send = call(
        top_kernel, pk, [*last, held, got], [two, two], work((4 * node, node), (4 * node, cols))
    )
    held, send = call(turn_kernel, pk, [keep, swap(send, "cube", 1)], [two, two])
    got = swap(send, "cube", 2)
    keep, send, top = call(
        down_kernel, pk, [*first, y1, held, got], [two, two, (rows, cols)], work(one, (2 * node, node))
    )
    got = swap(send, "cube", 1)
    (out,) = call(last_kernel, pk, [*first, y0, keep, got, top], [(3, rows, cols)], work(one))
    return out[:, None, None]


def from_partner(block, axis, apart):
    count = lax.axis_size(axis)
    route = []
    for low in range(count):
        high = low | 1 << apart
        if high != low and high < count:
            route += [(low, high), (high, low)]
    return lax.ppermute(block, axis, route)


def collect_pairs(residual_rows, tree_level, cube_index):
    gathered = residual_rows
    for bit_index in range(tree_level):
        partner_rows = from_partner(gathered, "cube", bit_index)
        lower_side = cube_index // 2**bit_index % 2 == 0
        gathered = jnp.where(
            lower_side,
            jnp.concatenate([gathered, partner_rows], axis=0),
            jnp.concatenate([partner_rows, gathered], axis=0),
        )
    return gathered


def reduce_pairs(partial_value, tree_level, cube_index):
    for bit_index in reversed(range(tree_level)):
        half_rows = partial_value.shape[0] // 2
        lower_rows = partial_value[:half_rows]
        upper_rows = partial_value[half_rows:]
        lower_side = cube_index // 2**bit_index % 2 == 0
        kept_rows = jnp.where(lower_side, lower_rows, upper_rows)
        sent_rows = jnp.where(lower_side, upper_rows, lower_rows)
        partial_value = kept_rows + from_partner(sent_rows, "cube", bit_index)
    return partial_value


def stepwise(right_side, diag_inverse, panels, extend_map):
    highest = lax.Precision.HIGHEST
    levels = right_side.shape[0]
    local_rows = right_side.shape[3]
    columns_k = right_side.shape[4]
    cube_index = lax.axis_index("cube")
    rhs_rows = right_side[:, 0, 0]
    panel_blocks = panels[:, 0, 0]
    row_maps = extend_map[:, 0, 0]
    row_ids = jnp.arange(local_rows, dtype=jnp.int32)
    update = jnp.zeros((local_rows, columns_k), jnp.float32)
    solved = []
    onehots = []
    diag_blocks = []
    for tree_level in range(levels):
        span_rows = 2**tree_level * local_rows
        offset = (2**tree_level - 1) * local_rows
        diag_block = diag_inverse[offset : offset + span_rows]
        diag_blocks.append(diag_block)
        residual_rows = rhs_rows[tree_level] - update
        column = collect_pairs(residual_rows, tree_level, cube_index)

        def term_rows(first_row, row_count, diag_block=diag_block, column=column):
            return jnp.einsum("ir,ik->rk", diag_block, column, precision=highest)

        solved_rows = lax.psum_scatter(
            term_rows(jnp.int32(0), lax.axis_size("blk") * local_rows),
            "blk",
            scatter_dimension=0,
            tiled=True,
        )
        solved.append(solved_rows)
        if tree_level + 1 < levels:
            onehot = (row_maps[tree_level][..., None] == row_ids).astype(jnp.float32)
            onehots.append(onehot)
            upd_rows = jnp.einsum(
                "hmr,rk->hmk", panel_blocks[tree_level], solved_rows, precision=highest
            )
            extended = jnp.einsum("hmt,hmk->htk", onehot, upd_rows, precision=highest)
            update = extended[0] + from_partner(extended[1], "cube", tree_level)
    results = [None] * levels
    parent = None
    for tree_level in reversed(range(levels)):
        span_rows = 2**tree_level * local_rows
        diag_block = diag_blocks[tree_level]
        work_rows = solved[tree_level]
        if parent is not None:
            partner_rows = from_partner(parent, "cube", tree_level)
            parent_pair = jnp.stack([parent, partner_rows], axis=0)
            fetched = jnp.einsum(
                "hmt,htk->hmk", onehots[tree_level], parent_pair, precision=highest
            )
            work_rows = work_rows - jnp.einsum(
                "hmr,hmk->rk", panel_blocks[tree_level], fetched, precision=highest
            )

        def accumulate(running, shard_rows, first_row, diag_block=diag_block):
            return jnp.einsum("ir,rk->ik", diag_block, shard_rows, precision=highest)

        initial = jnp.zeros((span_rows, columns_k), jnp.float32)
        partial_value = accumulate(
            initial, lax.all_gather(work_rows, "blk", axis=0, tiled=True), jnp.int32(0)
        )
        parent = reduce_pairs(partial_value, tree_level, cube_index)
        results[tree_level] = parent
    return jnp.stack(results)[:, None, None]

def body(right_side, diag_inverse, panels, extend_map):
    levels, _, _, rows, cols = right_side.shape
    n_blk = lax.axis_size("blk")
    pk = Packing(levels, rows, cols, diag_inverse.shape[1], n_blk)
    small = n_blk * diag_inverse.size * 4 <= GATHER_BYTES
    if levels == 3 and lax.axis_size("cube") == 4 and pk.fits and small:
        return gathered(pk, right_side, diag_inverse, panels, extend_map)
    return stepwise(right_side, diag_inverse, panels, extend_map)


def solution(mesh):
    placed = (
        P(None, "cube", "blk", None, None),
        P("cube", "blk"),
        P(None, "cube", "blk", None, None, None),
        P(None, "cube", "blk", None, None),
    )
    return jax.shard_map(
        body,
        mesh=mesh,
        in_specs=placed,
        out_specs=P(None, "cube", "blk", None, None),
        check_vma=False,
    )
```

```python
import functools

import jax
import jax.numpy as jnp
from jax import lax
from jax.experimental import pallas as pl
from jax.experimental.pallas import tpu as pltpu
from jax.sharding import PartitionSpec as P

GATHER_BYTES = 8 * 2**20


def split(a):
    high = a.astype(jnp.bfloat16)
    return high, (a - high.astype(jnp.float32)).astype(jnp.bfloat16)


def product(a, b, dims):
    (a_high, a_low), (b_high, b_low) = a, b
    return term(a_high, b_high, dims) + (term(a_high, b_low, dims) + term(a_low, b_high, dims))


def term(x, y, dims):
    return lax.dot_general(x, y, (dims, ((), ())), preferred_element_type=jnp.float32)


def dot_small(a, b):
    (a_high, a_low), (b_high, b_low) = split(a), split(b)
    return term(
        jnp.concatenate([a_high, a_high, a_low], axis=1),
        jnp.concatenate([b_high, b_low, b_high], axis=0),
        ((1,), (0,)),
    )


def dot_t_small(a, b):
    (a_high, a_low), (b_high, b_low) = split(a), split(b)
    return term(
        jnp.concatenate([a_high, a_high, a_low], axis=0),
        jnp.concatenate([b_high, b_low, b_high], axis=0),
        ((0,), (0,)),
    )


def swap(block, axis, mask):
    count = lax.axis_size(axis)
    return lax.ppermute(block, axis, [(i, i ^ mask) for i in range(count)])


def ring_place(blk, count):
    return jnp.where(blk % 2 == 0, blk // 2, count - 1 - blk // 2)


def ring_group(place, count):
    return jnp.where(place < count // 2, 2 * place, 2 * (count - 1 - place) + 1)


def ring_step(block, even, odd):
    cubes, count = lax.axis_size("cube"), lax.axis_size("blk")
    order = list(range(0, count, 2)) + list(range(count - 1, 0, -2))
    route = [
        (c * count + order[i], c * count + order[(i + (odd if c % 2 else even)) % count])
        for c in range(cubes)
        for i in range(count)
    ]
    return lax.ppermute(block, ("cube", "blk"), route)


def ring_offsets(count):
    return [0] + [x for r in range(1, count // 2) for x in (r, -r)] + [count // 2]


def gather_rows(block, AFTER={}):
    height = block.shape[0]
    moving = jnp.concatenate([block, swap(block, "cube", 1)], axis=0)
    out = [block]
    for r in range(1, lax.axis_size("blk") // 2):
        if r in AFTER:
            moving = tie(moving, AFTER[r])
        moving = ring_step(moving, 1, -1)
        out += [moving[:height], swap(moving[height:], "cube", 1)]
    if 4 in AFTER:
        moving = tie(moving, AFTER[4])
    return out + [ring_step(moving[:height], 1, -1)]


def gather_both_ways(block, JOINT=()):
    out = [block]
    up = down = block
    for r in range(1, lax.axis_size("blk") // 2):
        up, down = ring_step(up, 1, 1), ring_step(down, -1, -1)
        if r in JOINT:
            up, down = lax.optimization_barrier((up, down))
        out += [up, down]
    return out + [ring_step(up, 1, 1)]


class Packing:
    def __init__(self, levels, rows, cols, width, n_blk):
        self.levels, self.rows, self.cols, self.width, self.n_blk = levels, rows, cols, width, n_blk
        self.top = (2 ** (levels - 1) - 1) * rows
        self.low = (levels - 1) * (cols + 2 * rows)
        self.fold = width // cols
        self.fits = (
            self.low == width
            and width == n_blk * rows
            and rows % (8 * self.fold) == 0
            and n_blk == 2 ** (n_blk.bit_length() - 1)
        )
        self.height = self.top + rows + rows // self.fold

    def rhs(self, piece, level):
        rows, cols = self.rows, self.cols
        if level < self.levels - 1:
            return piece[self.top : self.top + rows, level * cols : (level + 1) * cols]
        start, step = self.top + rows, rows // self.fold
        return jnp.concatenate(
            [piece[start : start + step, j * cols : (j + 1) * cols] for j in range(self.fold)], axis=0
        )

    def extend(self, piece, level):
        first = (self.levels - 1) * self.cols + level * 2 * self.rows
        return piece[self.top : self.top + self.rows, first : first + 2 * self.rows]

    def diag(self, pieces, level, diag_ref, place_of, first=None):
        first = (2**level - 1) * self.rows if first is None else first
        for m, piece in enumerate(pieces):
            for p in range(2**level):
                diag_ref[place_of(self, m, p), :] = piece[first + p * self.rows : first + (p + 1) * self.rows, :]


def pack_kernel(pk, rhs_hbm, panels_hbm, maps_hbm, diag_hbm, out_ref, last_ref, rhs_ref, panels_ref, maps_ref, sems):
    rows = pk.rows
    pairs = [
        (rhs_hbm, rhs_ref),
        (panels_hbm, panels_ref),
        (maps_hbm, maps_ref),
        (diag_hbm.at[: pk.top], out_ref.at[: pk.top]),
        (diag_hbm.at[pk.top :], last_ref),
    ]
    copies = [pltpu.make_async_copy(a, b, sems.at[i]) for i, (a, b) in enumerate(pairs)]
    for copy in copies:
        copy.start()
    for copy in copies[:3]:
        copy.wait()
    parts = [rhs_ref[l, 0, 0] for l in range(pk.levels - 1)]
    for l in range(pk.levels - 1):
        for h in (0, 1):
            panel = panels_ref[l, 0, 0, h]
            row_ids = lax.broadcasted_iota(jnp.int32, (rows, panel.shape[0]), 0)
            names = maps_ref[l, 0, 0, h : h + 1, :]
            onehot = jnp.where(row_ids == names, 1.0, 0.0).astype(jnp.float32)
            parts.append(
                lax.dot_general(
                    panel,
                    onehot,
                    (((0,), (1,)), ((), ())),
                    precision=lax.Precision.HIGHEST,
                    preferred_element_type=jnp.float32,
                )
            )
    out_ref[pk.top : pk.top + rows, :] = jnp.concatenate(parts, axis=1)
    last = rhs_ref[pk.levels - 1, 0, 0]
    step = rows // pk.fold
    out_ref[pk.top + rows :, :] = jnp.concatenate(
        [last[j * step : (j + 1) * step] for j in range(pk.fold)], axis=1
    )
    for copy in copies[3:]:
        copy.wait()


def block_of(pk, m, p=0, side=1):
    count = pk.n_blk
    place = ring_place(lax.axis_index("blk"), count)
    group = ring_group((place - ring_offsets(count)[m] * side + count) % count, count)
    return pl.ds(pl.multiple_of(p * pk.width + group * pk.rows, pk.rows), pk.rows)


def shared_block_of(pk, m, p=0):
    return block_of(pk, m, p, 1 - 2 * (lax.axis_index("cube") % 2))


def extend_out(pk, level, pieces, y_ref, send_ref):
    rows, cols = pk.rows, pk.cols
    for m, piece in enumerate(pieces):
        place = block_of(pk, m)
        e = dot_t_small(pk.extend(piece, level), y_ref[place, :])
        send_ref[place, :cols] = pk.rhs(piece, level + 1) - e[:rows]
        send_ref[place, cols:] = e[rows:]


def split_kernel(pk, level, place_of, first, *refs):
    pieces, (high_ref, low_ref, diag_ref) = refs[: pk.n_blk], refs[pk.n_blk :]
    pk.diag(pieces, level, diag_ref, place_of, first)
    high_ref[...], low_ref[...] = split(diag_ref[...])


def first_kernel(pk, *refs):
    pieces, (send_ref, y_ref, diag_ref, z_ref) = refs[: pk.n_blk], refs[pk.n_blk :]
    pk.diag(pieces, 0, diag_ref, block_of)
    for m, piece in enumerate(pieces):
        z_ref[block_of(pk, m), :] = pk.rhs(piece, 0)
    y_ref[...] = product(split(diag_ref[...]), split(z_ref[...]), ((0,), (0,)))
    extend_out(pk, 0, pieces, y_ref, send_ref)


def middle_kernel(pk, *refs):
    pieces, (high_ref, low_ref, mine_ref, got_ref, send_ref, y_ref) = refs[: pk.n_blk], refs[pk.n_blk :]
    cols = pk.cols
    own = mine_ref[:, :cols] - got_ref[:, cols:]
    other = got_ref[:, :cols] - mine_ref[:, cols:]
    upper = lax.axis_index("cube") % 2 == 1
    z = jnp.concatenate([jnp.where(upper, other, own), jnp.where(upper, own, other)], axis=0)
    y_ref[...] = product((high_ref[...], low_ref[...]), split(z), ((0,), (0,)))
    extend_out(pk, 1, pieces, y_ref, send_ref)


def meet_kernel(pk, mine_ref, got_ref, out_ref):
    cols = pk.cols
    out_ref[:, :cols] = mine_ref[:, :cols] - got_ref[:, cols:]
    out_ref[:, cols:] = got_ref[:, :cols] - mine_ref[:, cols:]


def top_kernel(pk, high_ref, low_ref, mine_ref, got_ref, keep_ref, send_ref, vec_ref):
    node, cols = pk.width, pk.cols
    cube = lax.axis_index("cube")

    def part(k):
        return pl.ds(pl.multiple_of((cube ^ k) * node, node), node)

    vec_ref[part(0), :] = mine_ref[:, :cols]
    vec_ref[part(2), :] = mine_ref[:, cols:]
    vec_ref[part(1), :] = got_ref[:, :cols]
    vec_ref[part(3), :] = got_ref[:, cols:]
    diag = (high_ref[...], low_ref[...])
    y = product(diag, split(vec_ref[...]), ((0,), (0,)))
    vec_ref[...] = product(diag, split(y), ((1,), (0,)))
    keep_ref[:, :cols] = vec_ref[part(0), :]
    keep_ref[:, cols:] = vec_ref[part(2), :]
    send_ref[:, :cols] = vec_ref[part(1), :]
    send_ref[:, cols:] = vec_ref[part(3), :]


def turn_kernel(pk, mine_ref, got_ref, held_ref, send_ref):
    cols = pk.cols
    held = mine_ref[...] + got_ref[...]
    held_ref[...] = held
    send_ref[:, :cols] = held[:, cols:]
    send_ref[:, cols:] = held[:, :cols]


def reduce_rows(pk, level, pieces, y_ref, mine_ref, got_ref, w_ref):
    cols = pk.cols
    for m, piece in enumerate(pieces):
        place = block_of(pk, m)
        pair = mine_ref[place, :] + got_ref[place, :]
        both = jnp.concatenate([pair[:, :cols], pair[:, cols:]], axis=0)
        w_ref[place, :] = y_ref[place, :] - dot_small(pk.extend(piece, level), both)


def down_kernel(pk, *refs):
    pieces, refs = refs[: pk.n_blk], refs[pk.n_blk :]
    high_ref, low_ref, y_ref, mine_ref, got_ref, keep_ref, send_ref, top_ref, w_ref = refs
    node, cols = pk.width, pk.cols
    own_rows = block_of(pk, 0)
    top_ref[...] = mine_ref[own_rows, :cols] + got_ref[own_rows, :cols]
    reduce_rows(pk, 1, pieces, y_ref, mine_ref, got_ref, w_ref)
    x = product((high_ref[...], low_ref[...]), split(w_ref[...]), ((1,), (0,)))
    upper = lax.axis_index("cube") % 2 == 1
    own = jnp.where(upper, x[node:], x[:node])
    other = jnp.where(upper, x[:node], x[node:])
    keep_ref[:, :cols] = own
    keep_ref[:, cols:] = other
    send_ref[:, :cols] = other
    send_ref[:, cols:] = own


def last_kernel(pk, *refs):
    pieces, (y_ref, mine_ref, got_ref, top_ref, out_ref, w_ref) = refs[: pk.n_blk], refs[pk.n_blk :]
    cols = pk.cols
    own_rows = block_of(pk, 0)
    out_ref[2] = top_ref[...]
    out_ref[1] = mine_ref[own_rows, :cols] + got_ref[own_rows, :cols]
    reduce_rows(pk, 0, pieces, y_ref, mine_ref, got_ref, w_ref)
    out_ref[0] = product(split(pieces[0][: pk.rows, :]), split(w_ref[...]), ((1,), (0,)))


def call(kernel, pk, args, outs, scratch=(), place=pltpu.VMEM, room=24, kind=jnp.float32):
    return pl.pallas_call(
        functools.partial(kernel, pk),
        out_shape=[jax.ShapeDtypeStruct(s, kind) for s in outs],
        in_specs=[pl.BlockSpec(memory_space=place)] * len(args),
        out_specs=[pl.BlockSpec(memory_space=pltpu.VMEM)] * len(outs),
        scratch_shapes=scratch,
        compiler_params=pltpu.CompilerParams(vmem_limit_bytes=room * 2**20),
    )(*args)


def tie(value, other):
    return lax.optimization_barrier((value, other))[0]


def gathered(pk, right_side, diag_inverse, panels, extend_map):
    rows, cols, node = pk.rows, pk.cols, pk.width
    one, two = (node, cols), (node, 2 * cols)

    def work(*shapes):
        return [pltpu.VMEM(s, jnp.float32) for s in shapes]

    def split_diag(pieces, level, place_of, first):
        shape = (2**level * node, node)
        return call(
            lambda pk, *refs: split_kernel(pk, level, place_of, first, *refs),
            pk,
            pieces,
            [shape, shape],
            work(shape),
            kind=jnp.bfloat16,
        )

    inputs = [right_side, panels, extend_map, diag_inverse]
    packed, top = call(
        pack_kernel,
        pk,
        inputs,
        [(pk.height, node), (diag_inverse.shape[0] - pk.top, node)],
        [pltpu.VMEM(a.shape, a.dtype) for a in inputs[:3]]
        + [pltpu.SemaphoreType.DMA((5,))],
        pltpu.HBM,
        room=60,
    )
    first = gather_both_ways(packed, ())
    last = gather_rows(top, {})
    send, y0 = call(first_kernel, pk, first, [two, one], work((node, node), one))
    got = swap(send, "cube", 1)
    diag1 = split_diag(first, 1, block_of, None)
    send, y1 = call(middle_kernel, pk, [*first, *diag1, send, got], [two, one])
    got = tie(swap(send, "cube", 2), last[7])
    (held,) = call(meet_kernel, pk, [send, got], [two])
    got = swap(held, "cube", 1)
    diag2 = split_diag(last, 2, shared_block_of, 0)
    keep, send = call(top_kernel, pk, [*diag2, held, got], [two, two], work((4 * node, cols)))
    held, send = call(turn_kernel, pk, [keep, swap(send, "cube", 1)], [two, two])
    got = swap(send, "cube", 2)
    keep, send, top = call(
        down_kernel, pk, [*first, *diag1, y1, held, got], [two, two, (rows, cols)], work(one)
    )
    got = swap(send, "cube", 1)
    (out,) = call(last_kernel, pk, [*first, y0, keep, got, top], [(3, rows, cols)], work(one))
    return out[:, None, None]


def from_partner(block, axis, apart):
    count = lax.axis_size(axis)
    route = []
    for low in range(count):
        high = low | 1 << apart
        if high != low and high < count:
            route += [(low, high), (high, low)]
    return lax.ppermute(block, axis, route)


def collect_pairs(residual_rows, tree_level, cube_index):
    gathered = residual_rows
    for bit_index in range(tree_level):
        partner_rows = from_partner(gathered, "cube", bit_index)
        lower_side = cube_index // 2**bit_index % 2 == 0
        gathered = jnp.where(
            lower_side,
            jnp.concatenate([gathered, partner_rows], axis=0),
            jnp.concatenate([partner_rows, gathered], axis=0),
        )
    return gathered


def reduce_pairs(partial_value, tree_level, cube_index):
    for bit_index in reversed(range(tree_level)):
        half_rows = partial_value.shape[0] // 2
        lower_rows = partial_value[:half_rows]
        upper_rows = partial_value[half_rows:]
        lower_side = cube_index // 2**bit_index % 2 == 0
        kept_rows = jnp.where(lower_side, lower_rows, upper_rows)
        sent_rows = jnp.where(lower_side, upper_rows, lower_rows)
        partial_value = kept_rows + from_partner(sent_rows, "cube", bit_index)
    return partial_value


def stepwise(right_side, diag_inverse, panels, extend_map):
    highest = lax.Precision.HIGHEST
    levels = right_side.shape[0]
    local_rows = right_side.shape[3]
    columns_k = right_side.shape[4]
    cube_index = lax.axis_index("cube")
    rhs_rows = right_side[:, 0, 0]
    panel_blocks = panels[:, 0, 0]
    row_maps = extend_map[:, 0, 0]
    row_ids = jnp.arange(local_rows, dtype=jnp.int32)
    update = jnp.zeros((local_rows, columns_k), jnp.float32)
    solved = []
    onehots = []
    diag_blocks = []
    for tree_level in range(levels):
        span_rows = 2**tree_level * local_rows
        offset = (2**tree_level - 1) * local_rows
        diag_block = diag_inverse[offset : offset + span_rows]
        diag_blocks.append(diag_block)
        residual_rows = rhs_rows[tree_level] - update
        column = collect_pairs(residual_rows, tree_level, cube_index)

        def term_rows(first_row, row_count, diag_block=diag_block, column=column):
            return jnp.einsum("ir,ik->rk", diag_block, column, precision=highest)

        solved_rows = lax.psum_scatter(
            term_rows(jnp.int32(0), lax.axis_size("blk") * local_rows),
            "blk",
            scatter_dimension=0,
            tiled=True,
        )
        solved.append(solved_rows)
        if tree_level + 1 < levels:
            onehot = (row_maps[tree_level][..., None] == row_ids).astype(jnp.float32)
            onehots.append(onehot)
            upd_rows = jnp.einsum(
                "hmr,rk->hmk", panel_blocks[tree_level], solved_rows, precision=highest
            )
            extended = jnp.einsum("hmt,hmk->htk", onehot, upd_rows, precision=highest)
            update = extended[0] + from_partner(extended[1], "cube", tree_level)
    results = [None] * levels
    parent = None
    for tree_level in reversed(range(levels)):
        span_rows = 2**tree_level * local_rows
        diag_block = diag_blocks[tree_level]
        work_rows = solved[tree_level]
        if parent is not None:
            partner_rows = from_partner(parent, "cube", tree_level)
            parent_pair = jnp.stack([parent, partner_rows], axis=0)
            fetched = jnp.einsum(
                "hmt,htk->hmk", onehots[tree_level], parent_pair, precision=highest
            )
            work_rows = work_rows - jnp.einsum(
                "hmr,hmk->rk", panel_blocks[tree_level], fetched, precision=highest
            )

        def accumulate(running, shard_rows, first_row, diag_block=diag_block):
            return jnp.einsum("ir,rk->ik", diag_block, shard_rows, precision=highest)

        initial = jnp.zeros((span_rows, columns_k), jnp.float32)
        partial_value = accumulate(
            initial, lax.all_gather(work_rows, "blk", axis=0, tiled=True), jnp.int32(0)
        )
        parent = reduce_pairs(partial_value, tree_level, cube_index)
        results[tree_level] = parent
    return jnp.stack(results)[:, None, None]

def body(right_side, diag_inverse, panels, extend_map):
    levels, _, _, rows, cols = right_side.shape
    n_blk = lax.axis_size("blk")
    pk = Packing(levels, rows, cols, diag_inverse.shape[1], n_blk)
    small = n_blk * diag_inverse.size * 4 <= GATHER_BYTES
    if levels == 3 and lax.axis_size("cube") == 4 and pk.fits and small:
        return gathered(pk, right_side, diag_inverse, panels, extend_map)
    return stepwise(right_side, diag_inverse, panels, extend_map)


def solution(mesh):
    placed = (
        P(None, "cube", "blk", None, None),
        P("cube", "blk"),
        P(None, "cube", "blk", None, None, None),
        P(None, "cube", "blk", None, None),
    )
    return jax.shard_map(
        body,
        mesh=mesh,
        in_specs=placed,
        out_specs=P(None, "cube", "blk", None, None),
        check_vma=False,
    )
```

```python
import functools

import jax
import jax.numpy as jnp
from jax import lax
from jax.experimental import pallas as pl
from jax.experimental.pallas import tpu as pltpu
from jax.sharding import PartitionSpec as P

GATHER_BYTES = 8 * 2**20


def split(a):
    high = a.astype(jnp.bfloat16)
    return high, (a - high.astype(jnp.float32)).astype(jnp.bfloat16)


def product(a, b, dims):
    (a_high, a_low), (b_high, b_low) = a, b
    return term(a_high, b_high, dims) + (term(a_high, b_low, dims) + term(a_low, b_high, dims))


def term(x, y, dims):
    return lax.dot_general(x, y, (dims, ((), ())), preferred_element_type=jnp.float32)


def dot_small(a, b):
    (a_high, a_low), (b_high, b_low) = split(a), split(b)
    return term(
        jnp.concatenate([a_high, a_high, a_low], axis=1),
        jnp.concatenate([b_high, b_low, b_high], axis=0),
        ((1,), (0,)),
    )


def dot_t_small(a, b):
    (a_high, a_low), (b_high, b_low) = split(a), split(b)
    return term(
        jnp.concatenate([a_high, a_high, a_low], axis=0),
        jnp.concatenate([b_high, b_low, b_high], axis=0),
        ((0,), (0,)),
    )


def swap(block, axis, mask):
    count = lax.axis_size(axis)
    return lax.ppermute(block, axis, [(i, i ^ mask) for i in range(count)])


def ring_place(blk, count):
    return jnp.where(blk % 2 == 0, blk // 2, count - 1 - blk // 2)


def ring_group(place, count):
    return jnp.where(place < count // 2, 2 * place, 2 * (count - 1 - place) + 1)


def ring_step(block, even, odd):
    cubes, count = lax.axis_size("cube"), lax.axis_size("blk")
    order = list(range(0, count, 2)) + list(range(count - 1, 0, -2))
    route = [
        (c * count + order[i], c * count + order[(i + (odd if c % 2 else even)) % count])
        for c in range(cubes)
        for i in range(count)
    ]
    return lax.ppermute(block, ("cube", "blk"), route)


def ring_offsets(count):
    return [0] + [x for r in range(1, count // 2) for x in (r, -r)] + [count // 2]


def gather_rows(block):
    height = block.shape[0]
    even = lax.axis_index("cube") % 2 == 0
    up, down = ring_step(block, 1, 1), ring_step(block, -1, -1)
    out = [block, up, down]
    handed = swap(jnp.where(even, down, up), "cube", 1)
    moving = jnp.concatenate([jnp.where(even, up, down), handed], axis=0)
    for _ in range(2, lax.axis_size("blk") // 2):
        moving = ring_step(moving, 1, -1)
        out += [moving[:height], swap(moving[height:], "cube", 1)]
    return out + [ring_step(moving[:height], 1, -1)]


def gather_both_ways(block):
    out = [block]
    up = down = block
    for _ in range(1, lax.axis_size("blk") // 2):
        up, down = ring_step(up, 1, 1), ring_step(down, -1, -1)
        out += [up, down]
    return out + [ring_step(up, 1, 1)]


class Packing:
    def __init__(self, levels, rows, cols, width, n_blk):
        self.levels, self.rows, self.cols, self.width, self.n_blk = levels, rows, cols, width, n_blk
        self.top = (2 ** (levels - 1) - 1) * rows
        self.low = (levels - 1) * (cols + 2 * rows)
        self.fold = width // cols
        self.fits = (
            self.low == width
            and width == n_blk * rows
            and rows % (8 * self.fold) == 0
            and n_blk == 2 ** (n_blk.bit_length() - 1)
        )
        self.height = self.top + rows + rows // self.fold

    def rhs(self, piece, level):
        rows, cols = self.rows, self.cols
        if level < self.levels - 1:
            return piece[self.top : self.top + rows, level * cols : (level + 1) * cols]
        start, step = self.top + rows, rows // self.fold
        return jnp.concatenate(
            [piece[start : start + step, j * cols : (j + 1) * cols] for j in range(self.fold)], axis=0
        )

    def extend(self, piece, level):
        first = (self.levels - 1) * self.cols + level * 2 * self.rows
        return piece[self.top : self.top + self.rows, first : first + 2 * self.rows]

    def diag(self, pieces, level, diag_ref, place_of, first=None):
        first = (2**level - 1) * self.rows if first is None else first
        for m, piece in enumerate(pieces):
            for p in range(2**level):
                diag_ref[place_of(self, m, p), :] = piece[first + p * self.rows : first + (p + 1) * self.rows, :]


def pack_kernel(pk, rhs_hbm, panels_hbm, maps_hbm, diag_hbm, out_ref, last_ref, rhs_ref, panels_ref, maps_ref, sems):
    rows = pk.rows
    pairs = [
        (rhs_hbm, rhs_ref),
        (panels_hbm, panels_ref),
        (maps_hbm, maps_ref),
        (diag_hbm.at[: pk.top], out_ref.at[: pk.top]),
        (diag_hbm.at[pk.top :], last_ref),
    ]
    copies = [pltpu.make_async_copy(a, b, sems.at[i]) for i, (a, b) in enumerate(pairs)]
    for copy in copies:
        copy.start()
    for copy in copies[:3]:
        copy.wait()
    parts = [rhs_ref[l, 0, 0] for l in range(pk.levels - 1)]
    for l in range(pk.levels - 1):
        for h in (0, 1):
            panel = panels_ref[l, 0, 0, h]
            row_ids = lax.broadcasted_iota(jnp.int32, (rows, panel.shape[0]), 0)
            names = maps_ref[l, 0, 0, h : h + 1, :]
            onehot = jnp.where(row_ids == names, 1.0, 0.0).astype(jnp.float32)
            parts.append(
                lax.dot_general(
                    panel,
                    onehot,
                    (((0,), (1,)), ((), ())),
                    precision=lax.Precision.HIGHEST,
                    preferred_element_type=jnp.float32,
                )
            )
    out_ref[pk.top : pk.top + rows, :] = jnp.concatenate(parts, axis=1)
    last = rhs_ref[pk.levels - 1, 0, 0]
    step = rows // pk.fold
    out_ref[pk.top + rows :, :] = jnp.concatenate(
        [last[j * step : (j + 1) * step] for j in range(pk.fold)], axis=1
    )
    for copy in copies[3:]:
        copy.wait()


def block_of(pk, m, p=0, side=1):
    count = pk.n_blk
    place = ring_place(lax.axis_index("blk"), count)
    group = ring_group((place - ring_offsets(count)[m] * side + count) % count, count)
    return pl.ds(pl.multiple_of(p * pk.width + group * pk.rows, pk.rows), pk.rows)


def shared_block_of(pk, m, p=0):
    shared = 3 <= m < pk.n_blk - 1
    return block_of(pk, m, p, 1 - 2 * (lax.axis_index("cube") % 2) if shared else 1)


def extend_out(pk, level, pieces, y_ref, send_ref):
    rows, cols = pk.rows, pk.cols
    for m, piece in enumerate(pieces):
        place = block_of(pk, m)
        e = dot_t_small(pk.extend(piece, level), y_ref[place, :])
        send_ref[place, :cols] = pk.rhs(piece, level + 1) - e[:rows]
        send_ref[place, cols:] = e[rows:]


def split_kernel(pk, level, place_of, first, *refs):
    pieces, (high_ref, low_ref, diag_ref) = refs[: pk.n_blk], refs[pk.n_blk :]
    pk.diag(pieces, level, diag_ref, place_of, first)
    high_ref[...], low_ref[...] = split(diag_ref[...])


def first_kernel(pk, *refs):
    pieces, (send_ref, y_ref, diag_ref, z_ref) = refs[: pk.n_blk], refs[pk.n_blk :]
    pk.diag(pieces, 0, diag_ref, block_of)
    for m, piece in enumerate(pieces):
        z_ref[block_of(pk, m), :] = pk.rhs(piece, 0)
    y_ref[...] = product(split(diag_ref[...]), split(z_ref[...]), ((0,), (0,)))
    extend_out(pk, 0, pieces, y_ref, send_ref)


def middle_kernel(pk, *refs):
    pieces, (high_ref, low_ref, mine_ref, got_ref, send_ref, y_ref) = refs[: pk.n_blk], refs[pk.n_blk :]
    cols = pk.cols
    own = mine_ref[:, :cols] - got_ref[:, cols:]
    other = got_ref[:, :cols] - mine_ref[:, cols:]
    upper = lax.axis_index("cube") % 2 == 1
    z = jnp.concatenate([jnp.where(upper, other, own), jnp.where(upper, own, other)], axis=0)
    y_ref[...] = product((high_ref[...], low_ref[...]), split(z), ((0,), (0,)))
    extend_out(pk, 1, pieces, y_ref, send_ref)


def meet_kernel(pk, mine_ref, got_ref, out_ref):
    cols = pk.cols
    out_ref[:, :cols] = mine_ref[:, :cols] - got_ref[:, cols:]
    out_ref[:, cols:] = got_ref[:, :cols] - mine_ref[:, cols:]


def top_kernel(pk, high_ref, low_ref, mine_ref, got_ref, keep_ref, send_ref, vec_ref):
    node, cols = pk.width, pk.cols
    cube = lax.axis_index("cube")

    def part(k):
        return pl.ds(pl.multiple_of((cube ^ k) * node, node), node)

    vec_ref[part(0), :] = mine_ref[:, :cols]
    vec_ref[part(2), :] = mine_ref[:, cols:]
    vec_ref[part(1), :] = got_ref[:, :cols]
    vec_ref[part(3), :] = got_ref[:, cols:]
    diag = (high_ref[...], low_ref[...])
    y = product(diag, split(vec_ref[...]), ((0,), (0,)))
    vec_ref[...] = product(diag, split(y), ((1,), (0,)))
    keep_ref[:, :cols] = vec_ref[part(0), :]
    keep_ref[:, cols:] = vec_ref[part(2), :]
    send_ref[:, :cols] = vec_ref[part(1), :]
    send_ref[:, cols:] = vec_ref[part(3), :]


def turn_kernel(pk, mine_ref, got_ref, held_ref, send_ref):
    cols = pk.cols
    held = mine_ref[...] + got_ref[...]
    held_ref[...] = held
    send_ref[:, :cols] = held[:, cols:]
    send_ref[:, cols:] = held[:, :cols]


def reduce_rows(pk, level, pieces, y_ref, mine_ref, got_ref, w_ref):
    cols = pk.cols
    for m, piece in enumerate(pieces):
        place = block_of(pk, m)
        pair = mine_ref[place, :] + got_ref[place, :]
        both = jnp.concatenate([pair[:, :cols], pair[:, cols:]], axis=0)
        w_ref[place, :] = y_ref[place, :] - dot_small(pk.extend(piece, level), both)


def down_kernel(pk, *refs):
    pieces, refs = refs[: pk.n_blk], refs[pk.n_blk :]
    high_ref, low_ref, y_ref, mine_ref, got_ref, keep_ref, send_ref, top_ref, w_ref = refs
    node, cols = pk.width, pk.cols
    own_rows = block_of(pk, 0)
    top_ref[...] = mine_ref[own_rows, :cols] + got_ref[own_rows, :cols]
    reduce_rows(pk, 1, pieces, y_ref, mine_ref, got_ref, w_ref)
    x = product((high_ref[...], low_ref[...]), split(w_ref[...]), ((1,), (0,)))
    upper = lax.axis_index("cube") % 2 == 1
    own = jnp.where(upper, x[node:], x[:node])
    other = jnp.where(upper, x[:node], x[node:])
    keep_ref[:, :cols] = own
    keep_ref[:, cols:] = other
    send_ref[:, :cols] = other
    send_ref[:, cols:] = own


def last_kernel(pk, *refs):
    pieces, (y_ref, mine_ref, got_ref, top_ref, out_ref, w_ref) = refs[: pk.n_blk], refs[pk.n_blk :]
    cols = pk.cols
    own_rows = block_of(pk, 0)
    out_ref[2] = top_ref[...]
    out_ref[1] = mine_ref[own_rows, :cols] + got_ref[own_rows, :cols]
    reduce_rows(pk, 0, pieces, y_ref, mine_ref, got_ref, w_ref)
    out_ref[0] = product(split(pieces[0][: pk.rows, :]), split(w_ref[...]), ((1,), (0,)))


def call(kernel, pk, args, outs, scratch=(), place=pltpu.VMEM, room=24, kind=jnp.float32):
    return pl.pallas_call(
        functools.partial(kernel, pk),
        out_shape=[jax.ShapeDtypeStruct(s, kind) for s in outs],
        in_specs=[pl.BlockSpec(memory_space=place)] * len(args),
        out_specs=[pl.BlockSpec(memory_space=pltpu.VMEM)] * len(outs),
        scratch_shapes=scratch,
        compiler_params=pltpu.CompilerParams(vmem_limit_bytes=room * 2**20),
    )(*args)


def gathered(pk, right_side, diag_inverse, panels, extend_map):
    rows, cols, node = pk.rows, pk.cols, pk.width
    one, two = (node, cols), (node, 2 * cols)

    def work(*shapes):
        return [pltpu.VMEM(s, jnp.float32) for s in shapes]

    def split_diag(pieces, level, place_of, first):
        shape = (2**level * node, node)
        return call(
            lambda pk, *refs: split_kernel(pk, level, place_of, first, *refs),
            pk,
            pieces,
            [shape, shape],
            work(shape),
            kind=jnp.bfloat16,
        )

    inputs = [right_side, panels, extend_map, diag_inverse]
    packed, top = call(
        pack_kernel,
        pk,
        inputs,
        [(pk.height, node), (diag_inverse.shape[0] - pk.top, node)],
        [pltpu.VMEM(a.shape, a.dtype) for a in inputs[:3]]
        + [pltpu.SemaphoreType.DMA((5,))],
        pltpu.HBM,
        room=60,
    )
    first = gather_both_ways(packed)
    last = gather_rows(top)
    send, y0 = call(first_kernel, pk, first, [two, one], work((node, node), one))
    got = swap(send, "cube", 1)
    diag1 = split_diag(first, 1, block_of, None)
    send, y1 = call(middle_kernel, pk, [*first, *diag1, send, got], [two, one])
    got = swap(send, "cube", 2)
    (held,) = call(meet_kernel, pk, [send, got], [two])
    got = swap(held, "cube", 1)
    diag2 = split_diag(last, 2, shared_block_of, 0)
    keep, send = call(top_kernel, pk, [*diag2, held, got], [two, two], work((4 * node, cols)))
    held, send = call(turn_kernel, pk, [keep, swap(send, "cube", 1)], [two, two])
    got = swap(send, "cube", 2)
    keep, send, top = call(
        down_kernel, pk, [*first, *diag1, y1, held, got], [two, two, (rows, cols)], work(one)
    )
    got = swap(send, "cube", 1)
    (out,) = call(last_kernel, pk, [*first, y0, keep, got, top], [(3, rows, cols)], work(one))
    return out[:, None, None]


def from_partner(block, axis, apart):
    count = lax.axis_size(axis)
    route = []
    for low in range(count):
        high = low | 1 << apart
        if high != low and high < count:
            route += [(low, high), (high, low)]
    return lax.ppermute(block, axis, route)


def collect_pairs(residual_rows, tree_level, cube_index):
    gathered = residual_rows
    for bit_index in range(tree_level):
        partner_rows = from_partner(gathered, "cube", bit_index)
        lower_side = cube_index // 2**bit_index % 2 == 0
        gathered = jnp.where(
            lower_side,
            jnp.concatenate([gathered, partner_rows], axis=0),
            jnp.concatenate([partner_rows, gathered], axis=0),
        )
    return gathered


def reduce_pairs(partial_value, tree_level, cube_index):
    for bit_index in reversed(range(tree_level)):
        half_rows = partial_value.shape[0] // 2
        lower_rows = partial_value[:half_rows]
        upper_rows = partial_value[half_rows:]
        lower_side = cube_index // 2**bit_index % 2 == 0
        kept_rows = jnp.where(lower_side, lower_rows, upper_rows)
        sent_rows = jnp.where(lower_side, upper_rows, lower_rows)
        partial_value = kept_rows + from_partner(sent_rows, "cube", bit_index)
    return partial_value


def stepwise(right_side, diag_inverse, panels, extend_map):
    highest = lax.Precision.HIGHEST
    levels = right_side.shape[0]
    local_rows = right_side.shape[3]
    columns_k = right_side.shape[4]
    cube_index = lax.axis_index("cube")
    rhs_rows = right_side[:, 0, 0]
    panel_blocks = panels[:, 0, 0]
    row_maps = extend_map[:, 0, 0]
    row_ids = jnp.arange(local_rows, dtype=jnp.int32)
    update = jnp.zeros((local_rows, columns_k), jnp.float32)
    solved = []
    onehots = []
    diag_blocks = []
    for tree_level in range(levels):
        span_rows = 2**tree_level * local_rows
        offset = (2**tree_level - 1) * local_rows
        diag_block = diag_inverse[offset : offset + span_rows]
        diag_blocks.append(diag_block)
        residual_rows = rhs_rows[tree_level] - update
        column = collect_pairs(residual_rows, tree_level, cube_index)

        def term_rows(first_row, row_count, diag_block=diag_block, column=column):
            return jnp.einsum("ir,ik->rk", diag_block, column, precision=highest)

        solved_rows = lax.psum_scatter(
            term_rows(jnp.int32(0), lax.axis_size("blk") * local_rows),
            "blk",
            scatter_dimension=0,
            tiled=True,
        )
        solved.append(solved_rows)
        if tree_level + 1 < levels:
            onehot = (row_maps[tree_level][..., None] == row_ids).astype(jnp.float32)
            onehots.append(onehot)
            upd_rows = jnp.einsum(
                "hmr,rk->hmk", panel_blocks[tree_level], solved_rows, precision=highest
            )
            extended = jnp.einsum("hmt,hmk->htk", onehot, upd_rows, precision=highest)
            update = extended[0] + from_partner(extended[1], "cube", tree_level)
    results = [None] * levels
    parent = None
    for tree_level in reversed(range(levels)):
        span_rows = 2**tree_level * local_rows
        diag_block = diag_blocks[tree_level]
        work_rows = solved[tree_level]
        if parent is not None:
            partner_rows = from_partner(parent, "cube", tree_level)
            parent_pair = jnp.stack([parent, partner_rows], axis=0)
            fetched = jnp.einsum(
                "hmt,htk->hmk", onehots[tree_level], parent_pair, precision=highest
            )
            work_rows = work_rows - jnp.einsum(
                "hmr,hmk->rk", panel_blocks[tree_level], fetched, precision=highest
            )

        def accumulate(running, shard_rows, first_row, diag_block=diag_block):
            return jnp.einsum("ir,rk->ik", diag_block, shard_rows, precision=highest)

        initial = jnp.zeros((span_rows, columns_k), jnp.float32)
        partial_value = accumulate(
            initial, lax.all_gather(work_rows, "blk", axis=0, tiled=True), jnp.int32(0)
        )
        parent = reduce_pairs(partial_value, tree_level, cube_index)
        results[tree_level] = parent
    return jnp.stack(results)[:, None, None]

def body(right_side, diag_inverse, panels, extend_map):
    levels, _, _, rows, cols = right_side.shape
    n_blk = lax.axis_size("blk")
    pk = Packing(levels, rows, cols, diag_inverse.shape[1], n_blk)
    small = n_blk * diag_inverse.size * 4 <= GATHER_BYTES
    if levels == 3 and lax.axis_size("cube") == 4 and pk.fits and small:
        return gathered(pk, right_side, diag_inverse, panels, extend_map)
    return stepwise(right_side, diag_inverse, panels, extend_map)


def solution(mesh):
    placed = (
        P(None, "cube", "blk", None, None),
        P("cube", "blk"),
        P(None, "cube", "blk", None, None, None),
        P(None, "cube", "blk", None, None),
    )
    return jax.shard_map(
        body,
        mesh=mesh,
        in_specs=placed,
        out_specs=P(None, "cube", "blk", None, None),
        check_vma=False,
    )
```

```python
import functools

import jax
import jax.numpy as jnp
from jax import lax
from jax.experimental import pallas as pl
from jax.experimental.pallas import tpu as pltpu
from jax.sharding import PartitionSpec as P

GATHER_BYTES = 8 * 2**20


def split(a):
    high = a.astype(jnp.bfloat16)
    return high, (a - high.astype(jnp.float32)).astype(jnp.bfloat16)


def product(a, b, dims):
    (a_high, a_low), (b_high, b_low) = a, b
    return term(a_high, b_high, dims) + (term(a_high, b_low, dims) + term(a_low, b_high, dims))


def stacked_product(a, b, dims):
    high, low = split(a)
    both = term(jnp.concatenate([high, low], axis=0), b[0], dims)
    return both[: a.shape[0]] + both[a.shape[0] :] + term(high, b[1], dims)


def term(x, y, dims):
    return lax.dot_general(x, y, (dims, ((), ())), preferred_element_type=jnp.float32)


def dot_small(a, b):
    (a_high, a_low), (b_high, b_low) = split(a), split(b)
    return term(
        jnp.concatenate([a_high, a_high, a_low], axis=1),
        jnp.concatenate([b_high, b_low, b_high], axis=0),
        ((1,), (0,)),
    )


def dot_t_small(a, b):
    (a_high, a_low), (b_high, b_low) = split(a), split(b)
    return term(
        jnp.concatenate([a_high, a_high, a_low], axis=0),
        jnp.concatenate([b_high, b_low, b_high], axis=0),
        ((0,), (0,)),
    )


def swap(block, axis, mask):
    count = lax.axis_size(axis)
    return lax.ppermute(block, axis, [(i, i ^ mask) for i in range(count)])


def ring_place(blk, count):
    return jnp.where(blk % 2 == 0, blk // 2, count - 1 - blk // 2)


def ring_group(place, count):
    return jnp.where(place < count // 2, 2 * place, 2 * (count - 1 - place) + 1)


def ring_step(block, even, odd):
    cubes, count = lax.axis_size("cube"), lax.axis_size("blk")
    order = list(range(0, count, 2)) + list(range(count - 1, 0, -2))
    route = [
        (c * count + order[i], c * count + order[(i + (odd if c % 2 else even)) % count])
        for c in range(cubes)
        for i in range(count)
    ]
    return lax.ppermute(block, ("cube", "blk"), route)


def ring_offsets(count):
    return [0] + [x for r in range(1, count // 2) for x in (r, -r)] + [count // 2]


def gather_rows(block):
    height = block.shape[0]
    even = lax.axis_index("cube") % 2 == 0
    up, down = ring_step(block, 1, 1), ring_step(block, -1, -1)
    out = [block, up, down]
    handed = swap(jnp.where(even, down, up), "cube", 1)
    moving = jnp.concatenate([jnp.where(even, up, down), handed], axis=0)
    for _ in range(2, lax.axis_size("blk") // 2):
        moving = ring_step(moving, 1, -1)
        out += [moving[:height], swap(moving[height:], "cube", 1)]
    return out + [ring_step(moving[:height], 1, -1)]


def gather_both_ways(block):
    out = [block]
    up = down = block
    for _ in range(1, lax.axis_size("blk") // 2):
        up, down = ring_step(up, 1, 1), ring_step(down, -1, -1)
        out += [up, down]
    return out + [ring_step(jnp.where(lax.axis_index("cube") % 2 == 0, up, down), 1, -1)]


class Packing:
    def __init__(self, levels, rows, cols, width, n_blk):
        self.levels, self.rows, self.cols, self.width, self.n_blk = levels, rows, cols, width, n_blk
        self.top = (2 ** (levels - 1) - 1) * rows
        self.low = (levels - 1) * (cols + 2 * rows)
        self.fold = width // cols
        self.fits = (
            self.low == width
            and width == n_blk * rows
            and rows % (8 * self.fold) == 0
            and n_blk == 2 ** (n_blk.bit_length() - 1)
        )
        self.height = self.top + rows + rows // self.fold

    def rhs(self, piece, level):
        rows, cols = self.rows, self.cols
        if level < self.levels - 1:
            return piece[self.top : self.top + rows, level * cols : (level + 1) * cols]
        start, step = self.top + rows, rows // self.fold
        return jnp.concatenate(
            [piece[start : start + step, j * cols : (j + 1) * cols] for j in range(self.fold)], axis=0
        )

    def extend(self, piece, level):
        first = (self.levels - 1) * self.cols + level * 2 * self.rows
        return piece[self.top : self.top + self.rows, first : first + 2 * self.rows]

    def diag(self, pieces, level, diag_ref, place_of, first=None):
        first = (2**level - 1) * self.rows if first is None else first
        for m, piece in enumerate(pieces):
            for p in range(2**level):
                diag_ref[place_of(self, m, p), :] = piece[first + p * self.rows : first + (p + 1) * self.rows, :]


def pack_kernel(pk, rhs_hbm, panels_hbm, maps_hbm, diag_hbm, out_ref, last_ref, rhs_ref, panels_ref, maps_ref, sems):
    rows = pk.rows
    pairs = [
        (rhs_hbm, rhs_ref),
        (panels_hbm, panels_ref),
        (maps_hbm, maps_ref),
        (diag_hbm.at[: pk.top], out_ref.at[: pk.top]),
        (diag_hbm.at[pk.top :], last_ref),
    ]
    copies = [pltpu.make_async_copy(a, b, sems.at[i]) for i, (a, b) in enumerate(pairs)]
    for copy in copies:
        copy.start()
    for copy in copies[:3]:
        copy.wait()
    parts = [rhs_ref[l, 0, 0] for l in range(pk.levels - 1)]
    for l in range(pk.levels - 1):
        for h in (0, 1):
            panel = panels_ref[l, 0, 0, h]
            row_ids = lax.broadcasted_iota(jnp.int32, (rows, panel.shape[0]), 0)
            names = maps_ref[l, 0, 0, h : h + 1, :]
            onehot = jnp.where(row_ids == names, 1.0, 0.0).astype(jnp.float32)
            parts.append(
                lax.dot_general(
                    panel,
                    onehot,
                    (((0,), (1,)), ((), ())),
                    precision=lax.Precision.HIGHEST,
                    preferred_element_type=jnp.float32,
                )
            )
    out_ref[pk.top : pk.top + rows, :] = jnp.concatenate(parts, axis=1)
    last = rhs_ref[pk.levels - 1, 0, 0]
    step = rows // pk.fold
    out_ref[pk.top + rows :, :] = jnp.concatenate(
        [last[j * step : (j + 1) * step] for j in range(pk.fold)], axis=1
    )
    for copy in copies[3:]:
        copy.wait()


def block_of(pk, m, p=0, side=1):
    count = pk.n_blk
    place = ring_place(lax.axis_index("blk"), count)
    group = ring_group((place - ring_offsets(count)[m] * side + count) % count, count)
    return pl.ds(pl.multiple_of(p * pk.width + group * pk.rows, pk.rows), pk.rows)


def shared_block_of(pk, m, p=0):
    shared = 3 <= m < pk.n_blk - 1
    return block_of(pk, m, p, 1 - 2 * (lax.axis_index("cube") % 2) if shared else 1)


def extend_out(pk, level, pieces, y_ref, send_ref):
    rows, cols = pk.rows, pk.cols
    for m, piece in enumerate(pieces):
        place = block_of(pk, m)
        e = dot_t_small(pk.extend(piece, level), y_ref[place, :])
        send_ref[place, :cols] = pk.rhs(piece, level + 1) - e[:rows]
        send_ref[place, cols:] = e[rows:]


def split_kernel(pk, level, place_of, first, *refs):
    pieces, (high_ref, low_ref, diag_ref) = refs[: pk.n_blk], refs[pk.n_blk :]
    pk.diag(pieces, level, diag_ref, place_of, first)
    high_ref[...], low_ref[...] = split(diag_ref[...])


def first_kernel(pk, *refs):
    pieces, (send_ref, y_ref, diag_ref, z_ref) = refs[: pk.n_blk], refs[pk.n_blk :]
    pk.diag(pieces, 0, diag_ref, block_of)
    for m, piece in enumerate(pieces):
        z_ref[block_of(pk, m), :] = pk.rhs(piece, 0)
    y_ref[...] = product(split(diag_ref[...]), split(z_ref[...]), ((0,), (0,)))
    extend_out(pk, 0, pieces, y_ref, send_ref)


def middle_kernel(pk, *refs):
    pieces, (high_ref, low_ref, mine_ref, got_ref, send_ref, y_ref) = refs[: pk.n_blk], refs[pk.n_blk :]
    cols = pk.cols
    own = mine_ref[:, :cols] - got_ref[:, cols:]
    other = got_ref[:, :cols] - mine_ref[:, cols:]
    upper = lax.axis_index("cube") % 2 == 1
    z = jnp.concatenate([jnp.where(upper, other, own), jnp.where(upper, own, other)], axis=0)
    y_ref[...] = product((high_ref[...], low_ref[...]), split(z), ((0,), (0,)))
    extend_out(pk, 1, pieces, y_ref, send_ref)


def meet_kernel(pk, mine_ref, got_ref, out_ref):
    cols = pk.cols
    out_ref[:, :cols] = mine_ref[:, :cols] - got_ref[:, cols:]
    out_ref[:, cols:] = got_ref[:, :cols] - mine_ref[:, cols:]


def top_kernel(pk, high_ref, low_ref, mine_ref, got_ref, keep_ref, send_ref, vec_ref):
    node, cols = pk.width, pk.cols
    cube = lax.axis_index("cube")

    def part(k):
        return pl.ds(pl.multiple_of((cube ^ k) * node, node), node)

    vec_ref[part(0), :] = mine_ref[:, :cols]
    vec_ref[part(2), :] = mine_ref[:, cols:]
    vec_ref[part(1), :] = got_ref[:, :cols]
    vec_ref[part(3), :] = got_ref[:, cols:]
    diag = (high_ref[...], low_ref[...])
    y = stacked_product(vec_ref[...].T, diag, ((1,), (0,)))
    vec_ref[...] = stacked_product(y, diag, ((1,), (1,))).T
    keep_ref[:, :cols] = vec_ref[part(0), :]
    keep_ref[:, cols:] = vec_ref[part(2), :]
    send_ref[:, :cols] = vec_ref[part(1), :]
    send_ref[:, cols:] = vec_ref[part(3), :]


def turn_kernel(pk, mine_ref, got_ref, held_ref, send_ref):
    cols = pk.cols
    held = mine_ref[...] + got_ref[...]
    held_ref[...] = held
    send_ref[:, :cols] = held[:, cols:]
    send_ref[:, cols:] = held[:, :cols]


def reduce_rows(pk, level, pieces, y_ref, mine_ref, got_ref, w_ref):
    cols = pk.cols
    for m, piece in enumerate(pieces):
        place = block_of(pk, m)
        pair = mine_ref[place, :] + got_ref[place, :]
        both = jnp.concatenate([pair[:, :cols], pair[:, cols:]], axis=0)
        w_ref[place, :] = y_ref[place, :] - dot_small(pk.extend(piece, level), both)


def down_kernel(pk, *refs):
    pieces, refs = refs[: pk.n_blk], refs[pk.n_blk :]
    high_ref, low_ref, y_ref, mine_ref, got_ref, keep_ref, send_ref, top_ref, w_ref = refs
    node, cols = pk.width, pk.cols
    own_rows = block_of(pk, 0)
    top_ref[...] = mine_ref[own_rows, :cols] + got_ref[own_rows, :cols]
    reduce_rows(pk, 1, pieces, y_ref, mine_ref, got_ref, w_ref)
    x = product((high_ref[...], low_ref[...]), split(w_ref[...]), ((1,), (0,)))
    upper = lax.axis_index("cube") % 2 == 1
    own = jnp.where(upper, x[node:], x[:node])
    other = jnp.where(upper, x[:node], x[node:])
    keep_ref[:, :cols] = own
    keep_ref[:, cols:] = other
    send_ref[:, :cols] = other
    send_ref[:, cols:] = own


def last_kernel(pk, *refs):
    pieces, (y_ref, mine_ref, got_ref, top_ref, out_ref, w_ref) = refs[: pk.n_blk], refs[pk.n_blk :]
    cols = pk.cols
    own_rows = block_of(pk, 0)
    out_ref[2] = top_ref[...]
    out_ref[1] = mine_ref[own_rows, :cols] + got_ref[own_rows, :cols]
    reduce_rows(pk, 0, pieces, y_ref, mine_ref, got_ref, w_ref)
    out_ref[0] = product(split(pieces[0][: pk.rows, :]), split(w_ref[...]), ((1,), (0,)))


def tie(value, other):
    return lax.optimization_barrier((value, other))[0]


def call(kernel, pk, args, outs, scratch=(), place=pltpu.VMEM, room=24, kind=jnp.float32):
    return pl.pallas_call(
        functools.partial(kernel, pk),
        out_shape=[jax.ShapeDtypeStruct(s, kind) for s in outs],
        in_specs=[pl.BlockSpec(memory_space=place)] * len(args),
        out_specs=[pl.BlockSpec(memory_space=pltpu.VMEM)] * len(outs),
        scratch_shapes=scratch,
        compiler_params=pltpu.CompilerParams(vmem_limit_bytes=room * 2**20),
    )(*args)


def gathered(pk, right_side, diag_inverse, panels, extend_map):
    rows, cols, node = pk.rows, pk.cols, pk.width
    one, two = (node, cols), (node, 2 * cols)

    def work(*shapes):
        return [pltpu.VMEM(s, jnp.float32) for s in shapes]

    def split_diag(pieces, level, place_of, first):
        shape = (2**level * node, node)
        return call(
            lambda pk, *refs: split_kernel(pk, level, place_of, first, *refs),
            pk,
            pieces,
            [shape, shape],
            work(shape),
            kind=jnp.bfloat16,
        )

    inputs = [right_side, panels, extend_map, diag_inverse]
    packed, top = call(
        pack_kernel,
        pk,
        inputs,
        [(pk.height, node), (diag_inverse.shape[0] - pk.top, node)],
        [pltpu.VMEM(a.shape, a.dtype) for a in inputs[:3]]
        + [pltpu.SemaphoreType.DMA((5,))],
        pltpu.HBM,
        room=60,
    )
    first = gather_both_ways(packed)
    last = gather_rows(top)
    first[-1] = tie(first[-1], last[3])
    send, y0 = call(first_kernel, pk, first, [two, one], work((node, node), one))
    got = swap(send, "cube", 1)
    diag1 = split_diag(first, 1, block_of, None)
    send, y1 = call(middle_kernel, pk, [*first, *diag1, send, got], [two, one])
    got = swap(send, "cube", 2)
    (held,) = call(meet_kernel, pk, [send, got], [two])
    got = swap(held, "cube", 1)
    diag2 = split_diag(last, 2, shared_block_of, 0)
    keep, send = call(top_kernel, pk, [*diag2, held, got], [two, two], work((4 * node, cols)))
    held, send = call(turn_kernel, pk, [keep, swap(send, "cube", 1)], [two, two])
    got = swap(send, "cube", 2)
    keep, send, top = call(
        down_kernel, pk, [*first, *diag1, y1, held, got], [two, two, (rows, cols)], work(one)
    )
    got = swap(send, "cube", 1)
    (out,) = call(last_kernel, pk, [*first, y0, keep, got, top], [(3, rows, cols)], work(one))
    return out[:, None, None]


def from_partner(block, axis, apart):
    count = lax.axis_size(axis)
    route = []
    for low in range(count):
        high = low | 1 << apart
        if high != low and high < count:
            route += [(low, high), (high, low)]
    return lax.ppermute(block, axis, route)


def collect_pairs(residual_rows, tree_level, cube_index):
    gathered = residual_rows
    for bit_index in range(tree_level):
        partner_rows = from_partner(gathered, "cube", bit_index)
        lower_side = cube_index // 2**bit_index % 2 == 0
        gathered = jnp.where(
            lower_side,
            jnp.concatenate([gathered, partner_rows], axis=0),
            jnp.concatenate([partner_rows, gathered], axis=0),
        )
    return gathered


def reduce_pairs(partial_value, tree_level, cube_index):
    for bit_index in reversed(range(tree_level)):
        half_rows = partial_value.shape[0] // 2
        lower_rows = partial_value[:half_rows]
        upper_rows = partial_value[half_rows:]
        lower_side = cube_index // 2**bit_index % 2 == 0
        kept_rows = jnp.where(lower_side, lower_rows, upper_rows)
        sent_rows = jnp.where(lower_side, upper_rows, lower_rows)
        partial_value = kept_rows + from_partner(sent_rows, "cube", bit_index)
    return partial_value


def stepwise(right_side, diag_inverse, panels, extend_map):
    highest = lax.Precision.HIGHEST
    levels = right_side.shape[0]
    local_rows = right_side.shape[3]
    columns_k = right_side.shape[4]
    cube_index = lax.axis_index("cube")
    rhs_rows = right_side[:, 0, 0]
    panel_blocks = panels[:, 0, 0]
    row_maps = extend_map[:, 0, 0]
    row_ids = jnp.arange(local_rows, dtype=jnp.int32)
    update = jnp.zeros((local_rows, columns_k), jnp.float32)
    solved = []
    onehots = []
    diag_blocks = []
    for tree_level in range(levels):
        span_rows = 2**tree_level * local_rows
        offset = (2**tree_level - 1) * local_rows
        diag_block = diag_inverse[offset : offset + span_rows]
        diag_blocks.append(diag_block)
        residual_rows = rhs_rows[tree_level] - update
        column = collect_pairs(residual_rows, tree_level, cube_index)

        def term_rows(first_row, row_count, diag_block=diag_block, column=column):
            return jnp.einsum("ir,ik->rk", diag_block, column, precision=highest)

        solved_rows = lax.psum_scatter(
            term_rows(jnp.int32(0), lax.axis_size("blk") * local_rows),
            "blk",
            scatter_dimension=0,
            tiled=True,
        )
        solved.append(solved_rows)
        if tree_level + 1 < levels:
            onehot = (row_maps[tree_level][..., None] == row_ids).astype(jnp.float32)
            onehots.append(onehot)
            upd_rows = jnp.einsum(
                "hmr,rk->hmk", panel_blocks[tree_level], solved_rows, precision=highest
            )
            extended = jnp.einsum("hmt,hmk->htk", onehot, upd_rows, precision=highest)
            update = extended[0] + from_partner(extended[1], "cube", tree_level)
    results = [None] * levels
    parent = None
    for tree_level in reversed(range(levels)):
        span_rows = 2**tree_level * local_rows
        diag_block = diag_blocks[tree_level]
        work_rows = solved[tree_level]
        if parent is not None:
            partner_rows = from_partner(parent, "cube", tree_level)
            parent_pair = jnp.stack([parent, partner_rows], axis=0)
            fetched = jnp.einsum(
                "hmt,htk->hmk", onehots[tree_level], parent_pair, precision=highest
            )
            work_rows = work_rows - jnp.einsum(
                "hmr,hmk->rk", panel_blocks[tree_level], fetched, precision=highest
            )

        def accumulate(running, shard_rows, first_row, diag_block=diag_block):
            return jnp.einsum("ir,rk->ik", diag_block, shard_rows, precision=highest)

        initial = jnp.zeros((span_rows, columns_k), jnp.float32)
        partial_value = accumulate(
            initial, lax.all_gather(work_rows, "blk", axis=0, tiled=True), jnp.int32(0)
        )
        parent = reduce_pairs(partial_value, tree_level, cube_index)
        results[tree_level] = parent
    return jnp.stack(results)[:, None, None]

def body(right_side, diag_inverse, panels, extend_map):
    levels, _, _, rows, cols = right_side.shape
    n_blk = lax.axis_size("blk")
    pk = Packing(levels, rows, cols, diag_inverse.shape[1], n_blk)
    small = n_blk * diag_inverse.size * 4 <= GATHER_BYTES
    if levels == 3 and lax.axis_size("cube") == 4 and pk.fits and small:
        return gathered(pk, right_side, diag_inverse, panels, extend_map)
    return stepwise(right_side, diag_inverse, panels, extend_map)


def solution(mesh):
    placed = (
        P(None, "cube", "blk", None, None),
        P("cube", "blk"),
        P(None, "cube", "blk", None, None, None),
        P(None, "cube", "blk", None, None),
    )
    return jax.shard_map(
        body,
        mesh=mesh,
        in_specs=placed,
        out_specs=P(None, "cube", "blk", None, None),
        check_vma=False,
    )
```

```python
import functools

import jax
import jax.numpy as jnp
from jax import lax
from jax.experimental import pallas as pl
from jax.experimental.pallas import tpu as pltpu
from jax.sharding import PartitionSpec as P

GATHER_BYTES = 8 * 2**20


def split(a):
    high = a.astype(jnp.bfloat16)
    return high, (a - high.astype(jnp.float32)).astype(jnp.bfloat16)


def product(a, b, dims):
    (a_high, a_low), (b_high, b_low) = a, b
    return term(a_high, b_high, dims) + (term(a_high, b_low, dims) + term(a_low, b_high, dims))


def stacked_product(a, b, dims):
    high, low = split(a)
    both = term(jnp.concatenate([high, low], axis=0), b[0], dims)
    return both[: a.shape[0]] + both[a.shape[0] :] + term(high, b[1], dims)


def term(x, y, dims):
    return lax.dot_general(x, y, (dims, ((), ())), preferred_element_type=jnp.float32)


def dot_small(a, b):
    (a_high, a_low), (b_high, b_low) = split(a), split(b)
    return term(
        jnp.concatenate([a_high, a_high, a_low], axis=1),
        jnp.concatenate([b_high, b_low, b_high], axis=0),
        ((1,), (0,)),
    )


def dot_t_small(a, b):
    (a_high, a_low), (b_high, b_low) = split(a), split(b)
    return term(
        jnp.concatenate([a_high, a_high, a_low], axis=0),
        jnp.concatenate([b_high, b_low, b_high], axis=0),
        ((0,), (0,)),
    )


def swap(block, axis, mask):
    count = lax.axis_size(axis)
    return lax.ppermute(block, axis, [(i, i ^ mask) for i in range(count)])


def ring_place(blk, count):
    return jnp.where(blk % 2 == 0, blk // 2, count - 1 - blk // 2)


def ring_group(place, count):
    return jnp.where(place < count // 2, 2 * place, 2 * (count - 1 - place) + 1)


def ring_step(block, even, odd):
    cubes, count = lax.axis_size("cube"), lax.axis_size("blk")
    order = list(range(0, count, 2)) + list(range(count - 1, 0, -2))
    route = [
        (c * count + order[i], c * count + order[(i + (odd if c % 2 else even)) % count])
        for c in range(cubes)
        for i in range(count)
    ]
    return lax.ppermute(block, ("cube", "blk"), route)


def ring_offsets(count):
    return [0] + [x for r in range(1, count // 2) for x in (r, -r)] + [count // 2]


def gather_rows(block):
    height = block.shape[0]
    even = lax.axis_index("cube") % 2 == 0
    up, down = ring_step(block, 1, 1), ring_step(block, -1, -1)
    out = [block, up, down]
    handed = swap(jnp.where(even, down, up), "cube", 1)
    moving = jnp.concatenate([jnp.where(even, up, down), handed], axis=0)
    for _ in range(2, lax.axis_size("blk") // 2):
        moving = ring_step(moving, 1, -1)
        out += [moving[:height], swap(moving[height:], "cube", 1)]
    return out + [ring_step(moving[:height], 1, -1)]


def gather_both_ways(block):
    out = [block]
    up = down = block
    for _ in range(1, lax.axis_size("blk") // 2):
        up, down = ring_step(up, 1, 1), ring_step(down, -1, -1)
        out += [up, down]
    return out + [ring_step(jnp.where(lax.axis_index("cube") % 2 == 0, up, down), 1, -1)]


class Packing:
    def __init__(self, levels, rows, cols, width, n_blk):
        self.levels, self.rows, self.cols, self.width, self.n_blk = levels, rows, cols, width, n_blk
        self.top = (2 ** (levels - 1) - 1) * rows
        self.low = (levels - 1) * (cols + 2 * rows)
        self.fold = width // cols
        self.fits = (
            self.low == width
            and width == n_blk * rows
            and rows % (8 * self.fold) == 0
            and n_blk == 2 ** (n_blk.bit_length() - 1)
        )
        self.height = self.top + rows + rows // self.fold

    def rhs(self, piece, level):
        rows, cols = self.rows, self.cols
        if level < self.levels - 1:
            return piece[self.top : self.top + rows, level * cols : (level + 1) * cols]
        start, step = self.top + rows, rows // self.fold
        return jnp.concatenate(
            [piece[start : start + step, j * cols : (j + 1) * cols] for j in range(self.fold)], axis=0
        )

    def extend(self, piece, level):
        first = (self.levels - 1) * self.cols + level * 2 * self.rows
        return piece[self.top : self.top + self.rows, first : first + 2 * self.rows]

    def diag(self, pieces, level, diag_ref, place_of, first=None):
        first = (2**level - 1) * self.rows if first is None else first
        for m, piece in enumerate(pieces):
            for p in range(2**level):
                diag_ref[place_of(self, m, p), :] = piece[first + p * self.rows : first + (p + 1) * self.rows, :]


def pack_kernel(pk, rhs_hbm, panels_hbm, maps_hbm, diag_hbm, out_ref, last_ref, rhs_ref, panels_ref, maps_ref, sems):
    rows = pk.rows
    pairs = [
        (rhs_hbm, rhs_ref),
        (panels_hbm, panels_ref),
        (maps_hbm, maps_ref),
        (diag_hbm.at[: pk.top], out_ref.at[: pk.top]),
        (diag_hbm.at[pk.top :], last_ref),
    ]
    copies = [pltpu.make_async_copy(a, b, sems.at[i]) for i, (a, b) in enumerate(pairs)]
    for copy in copies:
        copy.start()
    for copy in copies[:3]:
        copy.wait()
    parts = [rhs_ref[l, 0, 0] for l in range(pk.levels - 1)]
    for l in range(pk.levels - 1):
        for h in (0, 1):
            panel = panels_ref[l, 0, 0, h]
            row_ids = lax.broadcasted_iota(jnp.int32, (rows, panel.shape[0]), 0)
            names = maps_ref[l, 0, 0, h : h + 1, :]
            onehot = jnp.where(row_ids == names, 1.0, 0.0).astype(jnp.float32)
            parts.append(
                lax.dot_general(
                    panel,
                    onehot,
                    (((0,), (1,)), ((), ())),
                    precision=lax.Precision.HIGHEST,
                    preferred_element_type=jnp.float32,
                )
            )
    out_ref[pk.top : pk.top + rows, :] = jnp.concatenate(parts, axis=1)
    last = rhs_ref[pk.levels - 1, 0, 0]
    step = rows // pk.fold
    out_ref[pk.top + rows :, :] = jnp.concatenate(
        [last[j * step : (j + 1) * step] for j in range(pk.fold)], axis=1
    )
    for copy in copies[3:]:
        copy.wait()


def block_of(pk, m, p=0, side=1):
    count = pk.n_blk
    place = ring_place(lax.axis_index("blk"), count)
    group = ring_group((place - ring_offsets(count)[m] * side + count) % count, count)
    return pl.ds(pl.multiple_of(p * pk.width + group * pk.rows, pk.rows), pk.rows)


def shared_block_of(pk, m, p=0):
    shared = 3 <= m < pk.n_blk - 1
    return block_of(pk, m, p, 1 - 2 * (lax.axis_index("cube") % 2) if shared else 1)


def extend_out(pk, level, pieces, y_ref, send_ref):
    rows, cols = pk.rows, pk.cols
    for m, piece in enumerate(pieces):
        place = block_of(pk, m)
        e = dot_t_small(pk.extend(piece, level), y_ref[place, :])
        send_ref[place, :cols] = pk.rhs(piece, level + 1) - e[:rows]
        send_ref[place, cols:] = e[rows:]


def split_kernel(pk, level, place_of, first, *refs):
    pieces, (high_ref, low_ref, diag_ref) = refs[: pk.n_blk], refs[pk.n_blk :]
    pk.diag(pieces, level, diag_ref, place_of, first)
    high_ref[...], low_ref[...] = split(diag_ref[...])


def first_kernel(pk, *refs):
    pieces, (send_ref, y_ref, diag_ref, z_ref) = refs[: pk.n_blk], refs[pk.n_blk :]
    pk.diag(pieces, 0, diag_ref, block_of)
    for m, piece in enumerate(pieces):
        z_ref[block_of(pk, m), :] = pk.rhs(piece, 0)
    y_ref[...] = stacked_product(z_ref[...].T, split(diag_ref[...]), ((1,), (0,))).T
    extend_out(pk, 0, pieces, y_ref, send_ref)


def middle_kernel(pk, *refs):
    pieces, (high_ref, low_ref, mine_ref, got_ref, send_ref, y_ref) = refs[: pk.n_blk], refs[pk.n_blk :]
    cols = pk.cols
    own = mine_ref[:, :cols] - got_ref[:, cols:]
    other = got_ref[:, :cols] - mine_ref[:, cols:]
    upper = lax.axis_index("cube") % 2 == 1
    z = jnp.concatenate([jnp.where(upper, other, own), jnp.where(upper, own, other)], axis=0)
    y_ref[...] = stacked_product(z.T, (high_ref[...], low_ref[...]), ((1,), (0,))).T
    extend_out(pk, 1, pieces, y_ref, send_ref)


def meet_kernel(pk, mine_ref, got_ref, out_ref):
    cols = pk.cols
    out_ref[:, :cols] = mine_ref[:, :cols] - got_ref[:, cols:]
    out_ref[:, cols:] = got_ref[:, :cols] - mine_ref[:, cols:]


def top_kernel(pk, high_ref, low_ref, mine_ref, got_ref, keep_ref, send_ref, vec_ref):
    node, cols = pk.width, pk.cols
    cube = lax.axis_index("cube")

    def part(k):
        return pl.ds(pl.multiple_of((cube ^ k) * node, node), node)

    vec_ref[part(0), :] = mine_ref[:, :cols]
    vec_ref[part(2), :] = mine_ref[:, cols:]
    vec_ref[part(1), :] = got_ref[:, :cols]
    vec_ref[part(3), :] = got_ref[:, cols:]
    diag = (high_ref[...], low_ref[...])
    y = stacked_product(vec_ref[...].T, diag, ((1,), (0,)))
    vec_ref[...] = stacked_product(y, diag, ((1,), (1,))).T
    keep_ref[:, :cols] = vec_ref[part(0), :]
    keep_ref[:, cols:] = vec_ref[part(2), :]
    send_ref[:, :cols] = vec_ref[part(1), :]
    send_ref[:, cols:] = vec_ref[part(3), :]


def turn_kernel(pk, mine_ref, got_ref, held_ref, send_ref):
    cols = pk.cols
    held = mine_ref[...] + got_ref[...]
    held_ref[...] = held
    send_ref[:, :cols] = held[:, cols:]
    send_ref[:, cols:] = held[:, :cols]


def reduce_rows(pk, level, pieces, y_ref, mine_ref, got_ref, w_ref):
    cols = pk.cols
    for m, piece in enumerate(pieces):
        place = block_of(pk, m)
        pair = mine_ref[place, :] + got_ref[place, :]
        both = jnp.concatenate([pair[:, :cols], pair[:, cols:]], axis=0)
        w_ref[place, :] = y_ref[place, :] - dot_small(pk.extend(piece, level), both)


def down_kernel(pk, *refs):
    pieces, refs = refs[: pk.n_blk], refs[pk.n_blk :]
    high_ref, low_ref, y_ref, mine_ref, got_ref, keep_ref, send_ref, top_ref, w_ref = refs
    node, cols = pk.width, pk.cols
    own_rows = block_of(pk, 0)
    top_ref[...] = mine_ref[own_rows, :cols] + got_ref[own_rows, :cols]
    reduce_rows(pk, 1, pieces, y_ref, mine_ref, got_ref, w_ref)
    x = stacked_product(w_ref[...].T, (high_ref[...], low_ref[...]), ((1,), (1,))).T
    upper = lax.axis_index("cube") % 2 == 1
    own = jnp.where(upper, x[node:], x[:node])
    other = jnp.where(upper, x[:node], x[node:])
    keep_ref[:, :cols] = own
    keep_ref[:, cols:] = other
    send_ref[:, :cols] = other
    send_ref[:, cols:] = own


def last_kernel(pk, *refs):
    pieces, (y_ref, mine_ref, got_ref, top_ref, out_ref, w_ref) = refs[: pk.n_blk], refs[pk.n_blk :]
    cols = pk.cols
    own_rows = block_of(pk, 0)
    out_ref[2] = top_ref[...]
    out_ref[1] = mine_ref[own_rows, :cols] + got_ref[own_rows, :cols]
    reduce_rows(pk, 0, pieces, y_ref, mine_ref, got_ref, w_ref)
    out_ref[0] = product(split(pieces[0][: pk.rows, :]), split(w_ref[...]), ((1,), (0,)))


def tie(value, other):
    return lax.optimization_barrier((value, other))[0]


def call(kernel, pk, args, outs, scratch=(), place=pltpu.VMEM, room=24, kind=jnp.float32):
    return pl.pallas_call(
        functools.partial(kernel, pk),
        out_shape=[jax.ShapeDtypeStruct(s, kind) for s in outs],
        in_specs=[pl.BlockSpec(memory_space=place)] * len(args),
        out_specs=[pl.BlockSpec(memory_space=pltpu.VMEM)] * len(outs),
        scratch_shapes=scratch,
        compiler_params=pltpu.CompilerParams(vmem_limit_bytes=room * 2**20),
    )(*args)


def gathered(pk, right_side, diag_inverse, panels, extend_map):
    rows, cols, node = pk.rows, pk.cols, pk.width
    one, two = (node, cols), (node, 2 * cols)

    def work(*shapes):
        return [pltpu.VMEM(s, jnp.float32) for s in shapes]

    def split_diag(pieces, level, place_of, first):
        shape = (2**level * node, node)
        return call(
            lambda pk, *refs: split_kernel(pk, level, place_of, first, *refs),
            pk,
            pieces,
            [shape, shape],
            work(shape),
            kind=jnp.bfloat16,
        )

    inputs = [right_side, panels, extend_map, diag_inverse]
    packed, top = call(
        pack_kernel,
        pk,
        inputs,
        [(pk.height, node), (diag_inverse.shape[0] - pk.top, node)],
        [pltpu.VMEM(a.shape, a.dtype) for a in inputs[:3]]
        + [pltpu.SemaphoreType.DMA((5,))],
        pltpu.HBM,
        room=60,
    )
    first = gather_both_ways(packed)
    last = gather_rows(top)
    first[-1] = tie(first[-1], last[3])
    send, y0 = call(first_kernel, pk, first, [two, one], work((node, node), one))
    got = swap(send, "cube", 1)
    diag1 = split_diag(first, 1, block_of, None)
    send, y1 = call(middle_kernel, pk, [*first, *diag1, send, got], [two, one])
    got = swap(send, "cube", 2)
    (held,) = call(meet_kernel, pk, [send, got], [two])
    got = swap(held, "cube", 1)
    diag2 = split_diag(last, 2, shared_block_of, 0)
    keep, send = call(top_kernel, pk, [*diag2, held, got], [two, two], work((4 * node, cols)))
    held, send = call(turn_kernel, pk, [keep, swap(send, "cube", 1)], [two, two])
    got = swap(send, "cube", 2)
    keep, send, top = call(
        down_kernel, pk, [*first, *diag1, y1, held, got], [two, two, (rows, cols)], work(one)
    )
    got = swap(send, "cube", 1)
    (out,) = call(last_kernel, pk, [*first, y0, keep, got, top], [(3, rows, cols)], work(one))
    return out[:, None, None]


def from_partner(block, axis, apart):
    count = lax.axis_size(axis)
    route = []
    for low in range(count):
        high = low | 1 << apart
        if high != low and high < count:
            route += [(low, high), (high, low)]
    return lax.ppermute(block, axis, route)


def collect_pairs(residual_rows, tree_level, cube_index):
    gathered = residual_rows
    for bit_index in range(tree_level):
        partner_rows = from_partner(gathered, "cube", bit_index)
        lower_side = cube_index // 2**bit_index % 2 == 0
        gathered = jnp.where(
            lower_side,
            jnp.concatenate([gathered, partner_rows], axis=0),
            jnp.concatenate([partner_rows, gathered], axis=0),
        )
    return gathered


def reduce_pairs(partial_value, tree_level, cube_index):
    for bit_index in reversed(range(tree_level)):
        half_rows = partial_value.shape[0] // 2
        lower_rows = partial_value[:half_rows]
        upper_rows = partial_value[half_rows:]
        lower_side = cube_index // 2**bit_index % 2 == 0
        kept_rows = jnp.where(lower_side, lower_rows, upper_rows)
        sent_rows = jnp.where(lower_side, upper_rows, lower_rows)
        partial_value = kept_rows + from_partner(sent_rows, "cube", bit_index)
    return partial_value


def stepwise(right_side, diag_inverse, panels, extend_map):
    highest = lax.Precision.HIGHEST
    levels = right_side.shape[0]
    local_rows = right_side.shape[3]
    columns_k = right_side.shape[4]
    cube_index = lax.axis_index("cube")
    rhs_rows = right_side[:, 0, 0]
    panel_blocks = panels[:, 0, 0]
    row_maps = extend_map[:, 0, 0]
    row_ids = jnp.arange(local_rows, dtype=jnp.int32)
    update = jnp.zeros((local_rows, columns_k), jnp.float32)
    solved = []
    onehots = []
    diag_blocks = []
    for tree_level in range(levels):
        span_rows = 2**tree_level * local_rows
        offset = (2**tree_level - 1) * local_rows
        diag_block = diag_inverse[offset : offset + span_rows]
        diag_blocks.append(diag_block)
        residual_rows = rhs_rows[tree_level] - update
        column = collect_pairs(residual_rows, tree_level, cube_index)

        def term_rows(first_row, row_count, diag_block=diag_block, column=column):
            return jnp.einsum("ir,ik->rk", diag_block, column, precision=highest)

        solved_rows = lax.psum_scatter(
            term_rows(jnp.int32(0), lax.axis_size("blk") * local_rows),
            "blk",
            scatter_dimension=0,
            tiled=True,
        )
        solved.append(solved_rows)
        if tree_level + 1 < levels:
            onehot = (row_maps[tree_level][..., None] == row_ids).astype(jnp.float32)
            onehots.append(onehot)
            upd_rows = jnp.einsum(
                "hmr,rk->hmk", panel_blocks[tree_level], solved_rows, precision=highest
            )
            extended = jnp.einsum("hmt,hmk->htk", onehot, upd_rows, precision=highest)
            update = extended[0] + from_partner(extended[1], "cube", tree_level)
    results = [None] * levels
    parent = None
    for tree_level in reversed(range(levels)):
        span_rows = 2**tree_level * local_rows
        diag_block = diag_blocks[tree_level]
        work_rows = solved[tree_level]
        if parent is not None:
            partner_rows = from_partner(parent, "cube", tree_level)
            parent_pair = jnp.stack([parent, partner_rows], axis=0)
            fetched = jnp.einsum(
                "hmt,htk->hmk", onehots[tree_level], parent_pair, precision=highest
            )
            work_rows = work_rows - jnp.einsum(
                "hmr,hmk->rk", panel_blocks[tree_level], fetched, precision=highest
            )

        def accumulate(running, shard_rows, first_row, diag_block=diag_block):
            return jnp.einsum("ir,rk->ik", diag_block, shard_rows, precision=highest)

        initial = jnp.zeros((span_rows, columns_k), jnp.float32)
        partial_value = accumulate(
            initial, lax.all_gather(work_rows, "blk", axis=0, tiled=True), jnp.int32(0)
        )
        parent = reduce_pairs(partial_value, tree_level, cube_index)
        results[tree_level] = parent
    return jnp.stack(results)[:, None, None]

def body(right_side, diag_inverse, panels, extend_map):
    levels, _, _, rows, cols = right_side.shape
    n_blk = lax.axis_size("blk")
    pk = Packing(levels, rows, cols, diag_inverse.shape[1], n_blk)
    small = n_blk * diag_inverse.size * 4 <= GATHER_BYTES
    if levels == 3 and lax.axis_size("cube") == 4 and pk.fits and small:
        return gathered(pk, right_side, diag_inverse, panels, extend_map)
    return stepwise(right_side, diag_inverse, panels, extend_map)


def solution(mesh):
    placed = (
        P(None, "cube", "blk", None, None),
        P("cube", "blk"),
        P(None, "cube", "blk", None, None, None),
        P(None, "cube", "blk", None, None),
    )
    return jax.shard_map(
        body,
        mesh=mesh,
        in_specs=placed,
        out_specs=P(None, "cube", "blk", None, None),
        check_vma=False,
    )
```

```python
import functools

import jax
import jax.numpy as jnp
from jax import lax
from jax.experimental import pallas as pl
from jax.experimental.pallas import tpu as pltpu
from jax.sharding import PartitionSpec as P

GATHER_BYTES = 8 * 2**20


def split(a):
    high = a.astype(jnp.bfloat16)
    return high, (a - high.astype(jnp.float32)).astype(jnp.bfloat16)


def product(a, b, dims):
    (a_high, a_low), (b_high, b_low) = a, b
    return term(a_high, b_high, dims) + (term(a_high, b_low, dims) + term(a_low, b_high, dims))


def stacked_product(a, b, dims):
    high, low = split(a)
    both = term(jnp.concatenate([high, low], axis=0), b[0], dims)
    return both[: a.shape[0]] + both[a.shape[0] :] + term(high, b[1], dims)


def term(x, y, dims):
    return lax.dot_general(x, y, (dims, ((), ())), preferred_element_type=jnp.float32)


def dot_small(a, b):
    (a_high, a_low), (b_high, b_low) = split(a), split(b)
    return term(
        jnp.concatenate([a_high, a_high, a_low], axis=1),
        jnp.concatenate([b_high, b_low, b_high], axis=0),
        ((1,), (0,)),
    )


def dot_t_small(a, b):
    (a_high, a_low), (b_high, b_low) = split(a), split(b)
    return term(
        jnp.concatenate([a_high, a_high, a_low], axis=0),
        jnp.concatenate([b_high, b_low, b_high], axis=0),
        ((0,), (0,)),
    )


def swap(block, axis, mask):
    count = lax.axis_size(axis)
    return lax.ppermute(block, axis, [(i, i ^ mask) for i in range(count)])


def ring_place(blk, count):
    return jnp.where(blk % 2 == 0, blk // 2, count - 1 - blk // 2)


def ring_group(place, count):
    return jnp.where(place < count // 2, 2 * place, 2 * (count - 1 - place) + 1)


def ring_step(block, even, odd):
    cubes, count = lax.axis_size("cube"), lax.axis_size("blk")
    order = list(range(0, count, 2)) + list(range(count - 1, 0, -2))
    route = [
        (c * count + order[i], c * count + order[(i + (odd if c % 2 else even)) % count])
        for c in range(cubes)
        for i in range(count)
    ]
    return lax.ppermute(block, ("cube", "blk"), route)


def ring_offsets(count):
    return [0] + [x for r in range(1, count // 2) for x in (r, -r)] + [count // 2]


def gather_rows(block):
    height = block.shape[0]
    even = lax.axis_index("cube") % 2 == 0
    up, down = ring_step(block, 1, 1), ring_step(block, -1, -1)
    out = [block, up, down]
    handed = swap(jnp.where(even, down, up), "cube", 1)
    moving = jnp.concatenate([jnp.where(even, up, down), handed], axis=0)
    for _ in range(2, lax.axis_size("blk") // 2):
        moving = ring_step(moving, 1, -1)
        out += [moving[:height], swap(moving[height:], "cube", 1)]
    return out + [ring_step(moving[:height], 1, -1)]


def gather_both_ways(block):
    out = [block]
    up = down = block
    for _ in range(1, lax.axis_size("blk") // 2):
        up, down = ring_step(up, 1, 1), ring_step(down, -1, -1)
        out += [up, down]
    return out + [ring_step(jnp.where(lax.axis_index("cube") % 2 == 0, up, down), 1, -1)]


class Packing:
    def __init__(self, levels, rows, cols, width, n_blk):
        self.levels, self.rows, self.cols, self.width, self.n_blk = levels, rows, cols, width, n_blk
        self.top = (2 ** (levels - 1) - 1) * rows
        self.low = (levels - 1) * (cols + 2 * rows)
        self.fold = width // cols
        self.fits = (
            self.low == width
            and width == n_blk * rows
            and rows % (8 * self.fold) == 0
            and n_blk == 2 ** (n_blk.bit_length() - 1)
        )
        self.height = self.top + rows + rows // self.fold

    def rhs(self, piece, level):
        rows, cols = self.rows, self.cols
        if level < self.levels - 1:
            return piece[self.top : self.top + rows, level * cols : (level + 1) * cols]
        start, step = self.top + rows, rows // self.fold
        return jnp.concatenate(
            [piece[start : start + step, j * cols : (j + 1) * cols] for j in range(self.fold)], axis=0
        )

    def extend(self, piece, level):
        first = (self.levels - 1) * self.cols + level * 2 * self.rows
        return piece[self.top : self.top + self.rows, first : first + 2 * self.rows]

    def diag(self, pieces, level, diag_ref, place_of, first=None):
        first = (2**level - 1) * self.rows if first is None else first
        for m, piece in enumerate(pieces):
            for p in range(2**level):
                diag_ref[place_of(self, m, p), :] = piece[first + p * self.rows : first + (p + 1) * self.rows, :]


def pack_kernel(pk, rhs_hbm, panels_hbm, maps_hbm, diag_hbm, out_ref, last_ref, rhs_ref, panels_ref, maps_ref, sems):
    rows = pk.rows
    pairs = [
        (rhs_hbm, rhs_ref),
        (panels_hbm, panels_ref),
        (maps_hbm, maps_ref),
        (diag_hbm.at[: pk.top], out_ref.at[: pk.top]),
        (diag_hbm.at[pk.top :], last_ref),
    ]
    copies = [pltpu.make_async_copy(a, b, sems.at[i]) for i, (a, b) in enumerate(pairs)]
    for copy in copies:
        copy.start()
    for copy in copies[:3]:
        copy.wait()
    parts = [rhs_ref[l, 0, 0] for l in range(pk.levels - 1)]
    for l in range(pk.levels - 1):
        for h in (0, 1):
            panel = panels_ref[l, 0, 0, h]
            row_ids = lax.broadcasted_iota(jnp.int32, (rows, panel.shape[0]), 0)
            names = maps_ref[l, 0, 0, h : h + 1, :]
            onehot = jnp.where(row_ids == names, 1.0, 0.0).astype(jnp.float32)
            parts.append(
                lax.dot_general(
                    panel,
                    onehot,
                    (((0,), (1,)), ((), ())),
                    precision=lax.Precision.HIGHEST,
                    preferred_element_type=jnp.float32,
                )
            )
    out_ref[pk.top : pk.top + rows, :] = jnp.concatenate(parts, axis=1)
    last = rhs_ref[pk.levels - 1, 0, 0]
    step = rows // pk.fold
    out_ref[pk.top + rows :, :] = jnp.concatenate(
        [last[j * step : (j + 1) * step] for j in range(pk.fold)], axis=1
    )
    for copy in copies[3:]:
        copy.wait()


def block_of(pk, m, p=0, side=1):
    count = pk.n_blk
    place = ring_place(lax.axis_index("blk"), count)
    group = ring_group((place - ring_offsets(count)[m] * side + count) % count, count)
    return pl.ds(pl.multiple_of(p * pk.width + group * pk.rows, pk.rows), pk.rows)


def shared_block_of(pk, m, p=0):
    shared = 3 <= m < pk.n_blk - 1
    return block_of(pk, m, p, 1 - 2 * (lax.axis_index("cube") % 2) if shared else 1)


def extend_out(pk, level, pieces, y_ref, send_ref):
    rows, cols = pk.rows, pk.cols
    for m, piece in enumerate(pieces):
        place = block_of(pk, m)
        e = dot_t_small(pk.extend(piece, level), y_ref[place, :])
        send_ref[place, :cols] = pk.rhs(piece, level + 1) - e[:rows]
        send_ref[place, cols:] = e[rows:]


def split_kernel(pk, level, place_of, first, *refs):
    pieces, (high_ref, low_ref, diag_ref) = refs[: pk.n_blk], refs[pk.n_blk :]
    pk.diag(pieces, level, diag_ref, place_of, first)
    high_ref[...], low_ref[...] = split(diag_ref[...])


def first_kernel(pk, *refs):
    pieces, (send_ref, y_ref, diag_ref, z_ref) = refs[: pk.n_blk], refs[pk.n_blk :]
    pk.diag(pieces, 0, diag_ref, block_of)
    for m, piece in enumerate(pieces):
        z_ref[block_of(pk, m), :] = pk.rhs(piece, 0)
    y_ref[...] = stacked_product(z_ref[...].T, split(diag_ref[...]), ((1,), (0,))).T
    extend_out(pk, 0, pieces, y_ref, send_ref)


def middle_kernel(pk, *refs):
    pieces, (high_ref, low_ref, mine_ref, got_ref, send_ref, y_ref) = refs[: pk.n_blk], refs[pk.n_blk :]
    cols = pk.cols
    own = mine_ref[:, :cols] - got_ref[:, cols:]
    other = got_ref[:, :cols] - mine_ref[:, cols:]
    upper = lax.axis_index("cube") % 2 == 1
    z = jnp.concatenate([jnp.where(upper, other, own), jnp.where(upper, own, other)], axis=0)
    y_ref[...] = stacked_product(z.T, (high_ref[...], low_ref[...]), ((1,), (0,))).T
    extend_out(pk, 1, pieces, y_ref, send_ref)


def meet_kernel(pk, mine_ref, got_ref, out_ref):
    cols = pk.cols
    out_ref[:, :cols] = mine_ref[:, :cols] - got_ref[:, cols:]
    out_ref[:, cols:] = got_ref[:, :cols] - mine_ref[:, cols:]


def top_kernel(pk, high_ref, low_ref, mine_ref, got_ref, keep_ref, send_ref, vec_ref):
    node, cols = pk.width, pk.cols
    cube = lax.axis_index("cube")

    def part(k):
        return pl.ds(pl.multiple_of((cube ^ k) * node, node), node)

    vec_ref[part(0), :] = mine_ref[:, :cols]
    vec_ref[part(2), :] = mine_ref[:, cols:]
    vec_ref[part(1), :] = got_ref[:, :cols]
    vec_ref[part(3), :] = got_ref[:, cols:]
    diag = (high_ref[...], low_ref[...])
    y = stacked_product(vec_ref[...].T, diag, ((1,), (0,)))
    vec_ref[...] = stacked_product(y, diag, ((1,), (1,))).T
    keep_ref[:, :cols] = vec_ref[part(0), :]
    keep_ref[:, cols:] = vec_ref[part(2), :]
    send_ref[:, :cols] = vec_ref[part(1), :]
    send_ref[:, cols:] = vec_ref[part(3), :]


def turn_kernel(pk, mine_ref, got_ref, held_ref, send_ref):
    cols = pk.cols
    held = mine_ref[...] + got_ref[...]
    held_ref[...] = held
    send_ref[:, :cols] = held[:, cols:]
    send_ref[:, cols:] = held[:, :cols]


def reduce_rows(pk, level, pieces, y_ref, mine_ref, got_ref, w_ref):
    cols = pk.cols
    for m, piece in enumerate(pieces):
        place = block_of(pk, m)
        pair = mine_ref[place, :] + got_ref[place, :]
        both = jnp.concatenate([pair[:, :cols], pair[:, cols:]], axis=0)
        w_ref[place, :] = y_ref[place, :] - dot_small(pk.extend(piece, level), both)


def down_kernel(pk, *refs):
    pieces, refs = refs[: pk.n_blk], refs[pk.n_blk :]
    high_ref, low_ref, y_ref, mine_ref, got_ref, keep_ref, send_ref, top_ref, w_ref = refs
    node, cols = pk.width, pk.cols
    own_rows = block_of(pk, 0)
    top_ref[...] = mine_ref[own_rows, :cols] + got_ref[own_rows, :cols]
    reduce_rows(pk, 1, pieces, y_ref, mine_ref, got_ref, w_ref)
    x = stacked_product(w_ref[...].T, (high_ref[...], low_ref[...]), ((1,), (1,))).T
    upper = lax.axis_index("cube") % 2 == 1
    own = jnp.where(upper, x[node:], x[:node])
    other = jnp.where(upper, x[:node], x[node:])
    keep_ref[:, :cols] = own
    keep_ref[:, cols:] = other
    send_ref[:, :cols] = other
    send_ref[:, cols:] = own


def last_kernel(pk, *refs):
    pieces, (y_ref, mine_ref, got_ref, top_ref, out_ref, w_ref) = refs[: pk.n_blk], refs[pk.n_blk :]
    cols = pk.cols
    own_rows = block_of(pk, 0)
    out_ref[2] = top_ref[...]
    out_ref[1] = mine_ref[own_rows, :cols] + got_ref[own_rows, :cols]
    reduce_rows(pk, 0, pieces, y_ref, mine_ref, got_ref, w_ref)
    out_ref[0] = product(split(pieces[0][: pk.rows, :]), split(w_ref[...]), ((1,), (0,)))


def tie(value, other):
    return lax.optimization_barrier((value, other))[0]


def call(kernel, pk, args, outs, scratch=(), place=pltpu.VMEM, room=24, kind=jnp.float32):
    return pl.pallas_call(
        functools.partial(kernel, pk),
        out_shape=[jax.ShapeDtypeStruct(s, kind) for s in outs],
        in_specs=[pl.BlockSpec(memory_space=place)] * len(args),
        out_specs=[pl.BlockSpec(memory_space=pltpu.VMEM)] * len(outs),
        scratch_shapes=scratch,
        compiler_params=pltpu.CompilerParams(vmem_limit_bytes=room * 2**20),
    )(*args)


def gathered(pk, right_side, diag_inverse, panels, extend_map):
    rows, cols, node = pk.rows, pk.cols, pk.width
    one, two = (node, cols), (node, 2 * cols)

    def work(*shapes):
        return [pltpu.VMEM(s, jnp.float32) for s in shapes]

    def split_diag(pieces, level, place_of, first):
        shape = (2**level * node, node)
        return call(
            lambda pk, *refs: split_kernel(pk, level, place_of, first, *refs),
            pk,
            pieces,
            [shape, shape],
            work(shape),
            kind=jnp.bfloat16,
        )

    inputs = [right_side, panels, extend_map, diag_inverse]
    packed, top = call(
        pack_kernel,
        pk,
        inputs,
        [(pk.height, node), (diag_inverse.shape[0] - pk.top, node)],
        [pltpu.VMEM(a.shape, a.dtype) for a in inputs[:3]]
        + [pltpu.SemaphoreType.DMA((5,))],
        pltpu.HBM,
        room=60,
    )
    first = gather_both_ways(packed)
    last = gather_rows(top)
    send, y0 = call(first_kernel, pk, first, [two, one], work((node, node), one))
    got = tie(swap(send, "cube", 1), last[3])
    diag1 = split_diag(first, 1, block_of, None)
    send, y1 = call(middle_kernel, pk, [*first, *diag1, send, got], [two, one])
    got = tie(swap(send, "cube", 2), last[5])
    (held,) = call(meet_kernel, pk, [send, got], [two])
    got = swap(held, "cube", 1)
    diag2 = split_diag(last, 2, shared_block_of, 0)
    keep, send = call(top_kernel, pk, [*diag2, held, got], [two, two], work((4 * node, cols)))
    held, send = call(turn_kernel, pk, [keep, swap(send, "cube", 1)], [two, two])
    got = swap(send, "cube", 2)
    keep, send, top = call(
        down_kernel, pk, [*first, *diag1, y1, held, got], [two, two, (rows, cols)], work(one)
    )
    got = swap(send, "cube", 1)
    (out,) = call(last_kernel, pk, [*first, y0, keep, got, top], [(3, rows, cols)], work(one))
    return out[:, None, None]


def from_partner(block, axis, apart):
    count = lax.axis_size(axis)
    route = []
    for low in range(count):
        high = low | 1 << apart
        if high != low and high < count:
            route += [(low, high), (high, low)]
    return lax.ppermute(block, axis, route)


def collect_pairs(residual_rows, tree_level, cube_index):
    gathered = residual_rows
    for bit_index in range(tree_level):
        partner_rows = from_partner(gathered, "cube", bit_index)
        lower_side = cube_index // 2**bit_index % 2 == 0
        gathered = jnp.where(
            lower_side,
            jnp.concatenate([gathered, partner_rows], axis=0),
            jnp.concatenate([partner_rows, gathered], axis=0),
        )
    return gathered


def reduce_pairs(partial_value, tree_level, cube_index):
    for bit_index in reversed(range(tree_level)):
        half_rows = partial_value.shape[0] // 2
        lower_rows = partial_value[:half_rows]
        upper_rows = partial_value[half_rows:]
        lower_side = cube_index // 2**bit_index % 2 == 0
        kept_rows = jnp.where(lower_side, lower_rows, upper_rows)
        sent_rows = jnp.where(lower_side, upper_rows, lower_rows)
        partial_value = kept_rows + from_partner(sent_rows, "cube", bit_index)
    return partial_value


def stepwise(right_side, diag_inverse, panels, extend_map):
    highest = lax.Precision.HIGHEST
    levels = right_side.shape[0]
    local_rows = right_side.shape[3]
    columns_k = right_side.shape[4]
    cube_index = lax.axis_index("cube")
    rhs_rows = right_side[:, 0, 0]
    panel_blocks = panels[:, 0, 0]
    row_maps = extend_map[:, 0, 0]
    row_ids = jnp.arange(local_rows, dtype=jnp.int32)
    update = jnp.zeros((local_rows, columns_k), jnp.float32)
    solved = []
    onehots = []
    diag_blocks = []
    for tree_level in range(levels):
        span_rows = 2**tree_level * local_rows
        offset = (2**tree_level - 1) * local_rows
        diag_block = diag_inverse[offset : offset + span_rows]
        diag_blocks.append(diag_block)
        residual_rows = rhs_rows[tree_level] - update
        column = collect_pairs(residual_rows, tree_level, cube_index)

        def term_rows(first_row, row_count, diag_block=diag_block, column=column):
            return jnp.einsum("ir,ik->rk", diag_block, column, precision=highest)

        solved_rows = lax.psum_scatter(
            term_rows(jnp.int32(0), lax.axis_size("blk") * local_rows),
            "blk",
            scatter_dimension=0,
            tiled=True,
        )
        solved.append(solved_rows)
        if tree_level + 1 < levels:
            onehot = (row_maps[tree_level][..., None] == row_ids).astype(jnp.float32)
            onehots.append(onehot)
            upd_rows = jnp.einsum(
                "hmr,rk->hmk", panel_blocks[tree_level], solved_rows, precision=highest
            )
            extended = jnp.einsum("hmt,hmk->htk", onehot, upd_rows, precision=highest)
            update = extended[0] + from_partner(extended[1], "cube", tree_level)
    results = [None] * levels
    parent = None
    for tree_level in reversed(range(levels)):
        span_rows = 2**tree_level * local_rows
        diag_block = diag_blocks[tree_level]
        work_rows = solved[tree_level]
        if parent is not None:
            partner_rows = from_partner(parent, "cube", tree_level)
            parent_pair = jnp.stack([parent, partner_rows], axis=0)
            fetched = jnp.einsum(
                "hmt,htk->hmk", onehots[tree_level], parent_pair, precision=highest
            )
            work_rows = work_rows - jnp.einsum(
                "hmr,hmk->rk", panel_blocks[tree_level], fetched, precision=highest
            )

        def accumulate(running, shard_rows, first_row, diag_block=diag_block):
            return jnp.einsum("ir,rk->ik", diag_block, shard_rows, precision=highest)

        initial = jnp.zeros((span_rows, columns_k), jnp.float32)
        partial_value = accumulate(
            initial, lax.all_gather(work_rows, "blk", axis=0, tiled=True), jnp.int32(0)
        )
        parent = reduce_pairs(partial_value, tree_level, cube_index)
        results[tree_level] = parent
    return jnp.stack(results)[:, None, None]

def body(right_side, diag_inverse, panels, extend_map):
    levels, _, _, rows, cols = right_side.shape
    n_blk = lax.axis_size("blk")
    pk = Packing(levels, rows, cols, diag_inverse.shape[1], n_blk)
    small = n_blk * diag_inverse.size * 4 <= GATHER_BYTES
    if levels == 3 and lax.axis_size("cube") == 4 and pk.fits and small:
        return gathered(pk, right_side, diag_inverse, panels, extend_map)
    return stepwise(right_side, diag_inverse, panels, extend_map)


def solution(mesh):
    placed = (
        P(None, "cube", "blk", None, None),
        P("cube", "blk"),
        P(None, "cube", "blk", None, None, None),
        P(None, "cube", "blk", None, None),
    )
    return jax.shard_map(
        body,
        mesh=mesh,
        in_specs=placed,
        out_specs=P(None, "cube", "blk", None, None),
        check_vma=False,
    )
```
